128 devices in a mesh: stream: 16 (over x, z), tensor: 8 (over y, core).
Axes of the slice: x: 4, y: 4, z: 4, core: 2. Of those that a mesh axis runs over, the one named last changes fastest.
Arguments:
- hidden: bfloat16 [1024, 8192], P('stream', 'tensor'), may hold values from -600 to 600
- norm_gain: bfloat16 [8192], replicated, may hold values from 0.099609375 to 1.8984375
- head_weight: bfloat16 [8192, 128256], P(None, ('stream', 'tensor')), may hold values from -32 to 32
- floor_counts: int32 [128256], P(('stream', 'tensor')), may hold values from 1 to 7
- totals: int32 [1024], replicated, may hold values from 1048576 to 4194304
- targets: int32 [1024], replicated, may hold values from 0 to 128255
Outputs:
- cumulative: float32 [1024, 128256], P(None, ('stream', 'tensor'))
- code_bits: float32 [1024], replicated
The draws below stay inside these ranges and needn't reach their ends.
All inputs are finite; a program needn't handle non-finite values.
Results may differ from the reference program's by a relative error of at most 0.0003.
The reference program's roundings to bfloat16 on the way (of `normed`) count: a program that leaves them out, or rounds other values in their place, can miss the bound.
Values may be sent and summed in bfloat16 or wider, within the bound.
No kernel may reach another device: no remote copies, remote signals or barrier semaphores. Data moves between devices by JAX's collectives and lax.ppermute only.
A program may use at most 128 MiB of HBM per device.

```python
import jax
import jax.numpy as jnp
from jax import lax

D = 8192
V = 128256
TOK_DEV = 64
TOKENS = 1024


def common_anchors(key):
    return jnp.clip(jax.random.normal(jax.random.fold_in(key, 77), (8, D), jnp.float32), -6.0, 6.0)


def anchor_rows(values, base, row_scale, anchors):
    row_index = jnp.arange(TOKENS, dtype=jnp.int32)
    aligned = row_index % 16 == 3
    chosen = anchors[row_index // 16 % 8]
    strength = (0.6 + 0.2 * (row_index // 16 % 3).astype(jnp.float32))[:, None]
    anchored = row_scale * (strength * chosen + (1.0 - strength) * base)
    return jnp.where(aligned[:, None], anchored, values)


def anchor_columns(values, anchors, noise_key, scale):
    block_width = V // 8
    anchor_index = jnp.repeat(jnp.arange(8, dtype=jnp.int32), 2)
    second_col = jnp.arange(16, dtype=jnp.int32) % 2
    column_index = anchor_index * block_width + 5 + second_col * (block_width // 2)
    noise = jnp.clip(jax.random.normal(noise_key, (D, 16), jnp.float32), -6.0, 6.0) * scale
    factor = 1.0 - 0.01 * second_col.astype(jnp.float32)
    columns_new = 250.0 / D * anchors[anchor_index].T * factor[None, :] + noise
    return values.at[:, column_index].set(columns_new)


def draw_hidden(key, part):
    anchors = common_anchors(key)
    key = jax.random.fold_in(key, 1)
    first_key, second_key, third_key = jax.random.split(key, 3)
    row_scale = jnp.exp(jax.random.uniform(first_key, (TOKENS, 1), jnp.float32) * jnp.log(10.0))
    column_scale = jnp.exp(jax.random.uniform(second_key, (1, D), jnp.float32) * jnp.log(10.0))
    base = jnp.clip(jax.random.normal(third_key, (TOKENS, D), jnp.float32), -6.0, 6.0)
    values = base * row_scale * column_scale
    values = anchor_rows(values, base, row_scale, anchors)
    return values.astype(jnp.bfloat16)


def draw_head_weight(key, part):
    anchors = common_anchors(key)
    key = jax.random.fold_in(key, 2)
    first_key, second_key = jax.random.split(key, 2)
    scale = 3.0 / D ** 0.5
    values = jnp.clip(jax.random.normal(first_key, (D, V), jnp.float32), -6.0, 6.0) * scale
    values = anchor_columns(values, anchors, second_key, scale)
    return values.astype(jnp.bfloat16)


def draw_floor_counts(key, part):
    key = jax.random.fold_in(key, 3)
    entries = jnp.arange(V, dtype=jnp.int32)
    upper = 1 + 6 * entries // V
    extra = jax.random.randint(key, (V,), 0, upper)
    counts = 1 + extra
    return jnp.where(entries == V - 1, 7, counts).astype(jnp.int32)


def touch_ends(result, stream_key, low, high):
    shape = result.shape
    place = [jax.random.randint(jax.random.fold_in(stream_key, axis), (), 0, shape[axis]) for axis in range(len(shape))]
    result = result.at[tuple(place)].set(low)
    longest = shape.index(max(shape))
    place[longest] = (place[longest] + 1) % shape[longest]
    return result.at[tuple(place)].set(high)


def setup_inputs(seed: int = 0) -> dict:
    arg_keys = jax.random.split(jax.random.key(seed), 7)
    hidden = draw_hidden(jax.random.fold_in(arg_keys[6], 71), 0)
    norm_gain = jnp.clip(1.0 + 0.18 * jax.random.normal(arg_keys[1], (D,), jnp.float32), 0.099609375, 1.8984375).astype(jnp.bfloat16)
    head_weight = draw_head_weight(jax.random.fold_in(arg_keys[6], 71), 0)
    floor_counts = draw_floor_counts(jax.random.fold_in(arg_keys[6], 71), 0)
    totals = touch_ends(jax.random.randint(arg_keys[4], (TOKENS,), 1048576, 4194305), jax.random.fold_in(arg_keys[4], 1), 1048576, 4194304).astype(jnp.int32)
    targets = touch_ends(jax.random.randint(arg_keys[5], (TOKENS,), 0, V), jax.random.fold_in(arg_keys[5], 1), 0, V - 1).astype(jnp.int32)
    return {"hidden": hidden, "norm_gain": norm_gain, "head_weight": head_weight, "floor_counts": floor_counts, "totals": totals, "targets": targets}


epsilon = 1e-05

def reference(hidden, norm_gain, head_weight, floor_counts, totals, targets):
    widened = hidden.astype(jnp.float32)
    mean_square = lax.optimization_barrier(jnp.mean(widened * widened, axis=1, keepdims=True))
    normed = (widened * lax.rsqrt(mean_square + epsilon) * norm_gain.astype(jnp.float32)[None, :]).astype(jnp.bfloat16)
    floor_float = floor_counts.astype(jnp.float32)
    floor_sum = jnp.sum(floor_float)
    columns = jnp.arange(V, dtype=jnp.int32)

    def per_block(operands):
        block_rows, block_totals, block_targets = operands
        logits = jnp.dot(block_rows, head_weight, preferred_element_type=jnp.float32)
        row_peak = lax.optimization_barrier(jnp.max(logits, axis=1, keepdims=True))
        exponent = jnp.exp(logits - row_peak)
        probabilities = exponent / lax.optimization_barrier(jnp.sum(exponent, axis=1, keepdims=True))
        token_total = block_totals.astype(jnp.float32)[:, None]
        quantized = (floor_float[None, :] + probabilities * (token_total - floor_sum)) / token_total
        running = jnp.cumsum(quantized, axis=1)
        cumulative = jnp.concatenate([jnp.zeros((quantized.shape[0], 1), quantized.dtype), running[:, :-1]], axis=1)
        picked = lax.optimization_barrier(jnp.sum(jnp.where(columns[None, :] == block_targets[:, None], quantized, 0.0), axis=1))
        return (cumulative, -jnp.log2(picked))
    blocks = TOKENS // TOK_DEV
    cumulative, code_bits = lax.map(per_block, (normed.reshape(blocks, TOK_DEV, D), totals.reshape(blocks, TOK_DEV), targets.reshape(blocks, TOK_DEV)))
    return (cumulative.reshape(TOKENS, V), code_bits.reshape(TOKENS))
```

```python
import jax
import jax.numpy as jnp
from jax import lax
from jax.experimental import pallas as pl
from jax.experimental.pallas import tpu as pltpu
from jax.sharding import PartitionSpec as P

epsilon = 1e-05
STREAM, TENSOR = "stream", "tensor"
BOTH = (STREAM, TENSOR)
SIZES = {"x": 4, "z": 4, "y": 4, "c": 2}
STRIDES = {"x": 32, "z": 8, "y": 2, "c": 1}
ROWS = 8
VMEM = pl.BlockSpec(memory_space=pltpu.VMEM)


def coordinate(axis):
    index = lax.axis_index(STREAM) * 8 + lax.axis_index(TENSOR)
    return lax.rem(lax.div(index, STRIDES[axis]), SIZES[axis])


def shift(value, axis, hops):
    size, stride = SIZES[axis], STRIDES[axis]
    pairs = []
    for source in range(128):
        place = source // stride % size
        pairs.append((source, source + ((place + hops) % size - place) * stride))
    return lax.ppermute(value, BOTH, pairs)


def call(body, out_shape, name, inputs, vmem_mib=32, scratch=(), out_specs=VMEM, **rest):
    return pl.pallas_call(
        body,
        out_shape=out_shape,
        in_specs=[VMEM] * len(inputs),
        out_specs=out_specs,
        scratch_shapes=list(scratch),
        compiler_params=pltpu.CompilerParams(vmem_limit_bytes=vmem_mib << 20),
        name=name,
        **rest,
    )(*inputs)


def local_stats(logits, floors, targets, first_column):
    entries = logits.shape[0]

    def body(first_ref, logits_ref, floors_ref, targets_ref, stats_ref):
        floors = floors_ref[...]
        total = jnp.sum(floors, axis=0, keepdims=True)
        rows = lax.broadcasted_iota(jnp.int32, (entries, 128), 0)
        for j in range(ROWS):
            tile = logits_ref[:, j * 128:(j + 1) * 128]
            peak = jnp.max(tile, axis=0, keepdims=True)
            exponent = jnp.exp(tile - peak)
            hit = rows == targets_ref[j:j + 1, :] - first_ref[0]
            stats_ref[j:j + 1, :] = peak
            stats_ref[8 + j:9 + j, :] = jnp.sum(exponent, axis=0, keepdims=True)
            stats_ref[16 + j:17 + j, :] = jnp.sum(jnp.where(hit, exponent, 0.0), axis=0, keepdims=True)
            stats_ref[24 + j:25 + j, :] = jnp.sum(jnp.where(hit, floors, 0.0), axis=0, keepdims=True)
            stats_ref[32 + j:33 + j, :] = total

    return pl.pallas_call(
        body,
        out_shape=jax.ShapeDtypeStruct((40, 128), jnp.float32),
        in_specs=[pl.BlockSpec(memory_space=pltpu.SMEM), VMEM, VMEM, VMEM],
        out_specs=VMEM,
        compiler_params=pltpu.CompilerParams(vmem_limit_bytes=32 << 20),
        name="local_stats",
    )(first_column, logits, floors, targets)


def running_sums(logits, floors, stats):
    entries, tokens = logits.shape
    block = 256
    blocks = -(-entries // block)

    def body(logits_ref, floors_ref, stats_ref, sums_ref, floor_sums_ref, tail, floor_tail):
        below = lax.broadcasted_iota(jnp.int32, (block, block), 1)
        lower = (below < lax.broadcasted_iota(jnp.int32, (block, block), 0)).astype(jnp.bfloat16)
        carry = [jnp.zeros((1, 128), jnp.float32)] * (ROWS + 1)
        for b in range(blocks):
            start, size = b * block, min(block, entries - b * block)
            for j in range(ROWS + 1):
                lanes = slice(j * 128, (j + 1) * 128)
                if j < ROWS:
                    value = jnp.exp(logits_ref[start:start + size, lanes] - stats_ref[j:j + 1, :])
                else:
                    value = floors_ref[start:start + size, :]
                if size < block:
                    tail[...] = jnp.zeros_like(tail)
                    tail[:size, :] = value
                    value = tail[...]
                high = value.astype(jnp.bfloat16)
                low = (value - high.astype(jnp.float32)).astype(jnp.bfloat16)
                partial = (
                    jnp.dot(lower, high, preferred_element_type=jnp.float32)
                    + jnp.dot(lower, low, preferred_element_type=jnp.float32)
                    + carry[j]
                )
                if j < ROWS:
                    sums_ref[start:start + size, lanes] = partial[:size]
                else:
                    floor_sums_ref[start:start + size, :] = partial[:size]
                carry[j] = carry[j] + jnp.sum(value, axis=0, keepdims=True)

    return call(
        body,
        (
            jax.ShapeDtypeStruct((entries, tokens), jnp.float32),
            jax.ShapeDtypeStruct((entries, 128), jnp.float32),
        ),
        "running_sums",
        (logits, floors, stats),
        scratch=[pltpu.VMEM((block, 128), jnp.float32), pltpu.VMEM((block, 128), jnp.float32)],
        out_specs=(VMEM, VMEM),
        cost_estimate=pl.CostEstimate(flops=2 * 2 * 256 * 1024 * 1024, bytes_accessed=8 << 20, transcendentals=1 << 20),
    )


def join(axis, stats, before, last=None):
    size = SIZES[axis]
    pieces = [stats] + [shift(stats, axis, k) for k in range(1, size)]

    def body(*refs):
        piece_refs, before_ref = refs[:size], refs[size]
        rest = refs[size + 1:]
        held = rest[-1]
        mine = coordinate(axis)
        for k in range(size):
            held[lax.rem(mine - k + size, size)] = piece_refs[k][...]
        peak = held[0, 0:8]
        for i in range(1, size):
            peak = jnp.maximum(peak, held[i, 0:8])
        mass = target = floor = total = jnp.zeros((8, 128), jnp.float32)
        mass_before = before_ref[0:8] * jnp.exp(piece_refs[0][0:8] - peak)
        total_before = before_ref[8:16]
        for i in range(size):
            scale = jnp.exp(held[i, 0:8] - peak)
            part = held[i, 8:16] * scale
            mass = mass + part
            target = target + held[i, 16:24] * scale
            floor = floor + held[i, 24:32]
            total = total + held[i, 32:40]
            earlier = i < mine
            mass_before = mass_before + jnp.where(earlier, part, 0.0)
            total_before = total_before + jnp.where(earlier, held[i, 32:40], 0.0)
        if last is None:
            stats_ref, after_ref = rest[0], rest[1]
            stats_ref[0:8] = peak
            stats_ref[8:16] = mass
            stats_ref[16:24] = target
            stats_ref[24:32] = floor
            stats_ref[32:40] = total
            after_ref[0:8] = mass_before
            after_ref[8:16] = total_before
        else:
            own_ref, totals_ref, terms_ref, bits_ref = rest[:4]
            tokens = totals_ref[...].astype(jnp.float32)
            free = (tokens - total) / mass
            terms_ref[0:8] = jnp.exp(own_ref[0:8] - peak) * free / tokens
            terms_ref[8:16] = 1.0 / tokens
            terms_ref[16:24] = (total_before + mass_before * free) / tokens
            bits_ref[...] = -jnp.log2((floor + target * free) / tokens)

    inputs = pieces + [before] + ([] if last is None else list(last))
    first, second = ((40, 128), (16, 128)) if last is None else ((24, 128), (8, 128))
    return call(
        body,
        (jax.ShapeDtypeStruct(first, jnp.float32), jax.ShapeDtypeStruct(second, jnp.float32)),
        "join_" + axis,
        inputs,
        vmem_mib=4,
        scratch=[pltpu.VMEM((size, 40, 128), jnp.float32)],
        out_specs=(VMEM, VMEM),
    )


def finish(sums, floor_sums, terms):
    entries, tokens = sums.shape
    block = 168

    def body(sums_ref, floors_ref, terms_ref, out_ref):
        for j in range(ROWS):
            lanes = slice(j * 128, (j + 1) * 128)
            out_ref[:, lanes] = (
                sums_ref[:, lanes] * terms_ref[j:j + 1, :]
                + floors_ref[...] * terms_ref[8 + j:9 + j, :]
                + terms_ref[16 + j:17 + j, :]
            )

    return pl.pallas_call(
        body,
        grid=(-(-entries // block),),
        out_shape=jax.ShapeDtypeStruct((entries, tokens), jnp.float32),
        in_specs=[
            pl.BlockSpec((block, tokens), lambda i: (i, 0)),
            pl.BlockSpec((block, 128), lambda i: (i, 0)),
            pl.BlockSpec((24, 128), lambda i: (0, 0)),
        ],
        out_specs=pl.BlockSpec((block, tokens), lambda i: (i, 0)),
        compiler_params=pltpu.CompilerParams(vmem_limit_bytes=16 << 20),
        name="finish",
    )(sums, floor_sums, terms)


def outputs(logits, floor_counts, totals, targets):
    entries = logits.shape[0]
    floors = jnp.broadcast_to(floor_counts.astype(jnp.float32)[:, None], (entries, 128))
    first_column = (lax.axis_index(STREAM) * 8 + lax.axis_index(TENSOR)) * entries
    stats = local_stats(logits, floors, targets.reshape(8, 128), first_column.reshape(1))
    group, before = stats, jnp.zeros((16, 128), jnp.float32)
    sums, floor_sums = running_sums(logits, floors, stats)
    for axis in ("c", "y", "z"):
        group, before = join(axis, group, before)
    terms, bits = join("x", group, before, last=(stats, totals.reshape(8, 128)))
    cumulative = finish(sums, floor_sums, terms)
    return cumulative.T, bits.reshape(1024)


def normalize(features, norm_gain):
    widened = features.astype(jnp.float32)
    mean_square = jnp.mean(widened * widened, axis=1, keepdims=True)
    return (
        widened * lax.rsqrt(mean_square + epsilon) * norm_gain.astype(jnp.float32)[None, :]
    ).astype(jnp.bfloat16)


def local(hidden, norm_gain, head_weight, floor_counts, totals, targets):
    gathered = lax.all_gather(hidden, TENSOR, axis=1, tiled=True)
    normed = normalize(gathered, norm_gain)
    everyone = lax.all_gather(normed, STREAM, axis=0, tiled=True)
    logits = lax.dot_general(
        head_weight, everyone, (((0,), (1,)), ((), ())), preferred_element_type=jnp.float32
    )
    return outputs(logits, floor_counts, totals, targets)


def solution(mesh):
    in_specs = (
        P(STREAM, TENSOR),
        P(),
        P(None, BOTH),
        P(BOTH),
        P(),
        P(),
    )
    out_specs = (P(None, BOTH), P())
    return jax.shard_map(local, mesh=mesh, in_specs=in_specs, out_specs=out_specs, check_vma=False)
```

```python
import jax
import jax.numpy as jnp
from jax import lax
from jax.experimental import pallas as pl
from jax.experimental.pallas import tpu as pltpu
from jax.sharding import PartitionSpec as P

epsilon = 1e-05
STREAM, TENSOR = "stream", "tensor"
BOTH = (STREAM, TENSOR)
SIZES = {"x": 4, "z": 4, "y": 4, "c": 2}
STRIDES = {"x": 32, "z": 8, "y": 2, "c": 1}
ROWS = 8
VMEM = pl.BlockSpec(memory_space=pltpu.VMEM)


def coordinate(axis):
    index = lax.axis_index(STREAM) * 8 + lax.axis_index(TENSOR)
    return lax.rem(lax.div(index, STRIDES[axis]), SIZES[axis])


def shift(value, axis, hops):
    pairs = []
    for source in range(128):
        name = axis[source % len(axis)]
        size, stride = SIZES[name], STRIDES[name]
        place = source // stride % size
        pairs.append((source, source + ((place + hops) % size - place) * stride))
    return lax.ppermute(value, BOTH, pairs)


def call(body, out_shape, name, inputs, vmem_mib=32, scratch=(), out_specs=VMEM, **rest):
    return pl.pallas_call(
        body,
        out_shape=out_shape,
        in_specs=[VMEM] * len(inputs),
        out_specs=out_specs,
        scratch_shapes=list(scratch),
        compiler_params=pltpu.CompilerParams(vmem_limit_bytes=vmem_mib << 20),
        name=name,
        **rest,
    )(*inputs)


def prepare(floor_counts, gain, targets):
    entries = floor_counts.shape[1]

    def body(floors_ref, gain_ref, targets_ref, columns_ref, gain_out_ref, stats_ref, row):
        row[...] = jnp.zeros_like(row)
        row[:, 0:entries] = jnp.broadcast_to(floors_ref[...].astype(jnp.float32), (8, entries))
        total = jnp.zeros((1, 128), jnp.float32)
        picked = [jnp.zeros((1, 128), jnp.float32)] * ROWS
        for b in range(ROWS):
            columns = jnp.transpose(jnp.concatenate([row[:, b * 128:(b + 1) * 128]] * 16, axis=0))
            columns_ref[b * 128:(b + 1) * 128, :] = columns
            total = total + jnp.sum(columns, axis=0, keepdims=True)
            rows = lax.broadcasted_iota(jnp.int32, (128, 128), 0) + (b * 128 + first_entry(entries))
            for j in range(ROWS):
                hit = jnp.where(rows == targets_ref[j:j + 1, :], columns, 0.0)
                picked[j] = picked[j] + jnp.sum(hit, axis=0, keepdims=True)
        stats_ref[0:8] = jnp.concatenate(picked, axis=0)
        stats_ref[8:16] = jnp.broadcast_to(total, (8, 128))
        gain_out_ref[...] = gain_ref[...].astype(jnp.float32).reshape(1, 8192)

    return call(
        body,
        (
            jax.ShapeDtypeStruct((1024, 128), jnp.float32),
            jax.ShapeDtypeStruct((1, 8192), jnp.float32),
            jax.ShapeDtypeStruct((16, 128), jnp.float32),
        ),
        "prepare",
        (floor_counts, gain, targets),
        vmem_mib=4,
        scratch=[pltpu.VMEM((8, 1024), jnp.float32)],
        out_specs=(VMEM, VMEM, VMEM),
    )


def first_entry(entries):
    return (lax.axis_index(STREAM) * 8 + lax.axis_index(TENSOR)) * entries


def join_halves(products, floor_stats, targets):
    entries = products.shape[2]

    def body(products_ref, floors_ref, targets_ref, logits_ref, stats_ref):
        core = lax.rem(lax.axis_index(TENSOR), 2)
        first = first_entry(entries)
        rows = lax.broadcasted_iota(jnp.int32, (entries, 128), 0)
        left = lax.broadcasted_iota(jnp.int32, (entries, 128), 1) < 64
        logits_ref[1000:1024, :] = jnp.full((24, 1024), -jnp.inf, jnp.float32)
        for j in range(ROWS):
            x, z = j // 2, j % 2 * 2
            near = slice(x // 2 * 128, x // 2 * 128 + 128)
            one, two = products_ref[core, z, :, near], products_ref[core, z + 1, :, near]
            if x % 2 == 0:
                two = pltpu.roll(two, 64, 1)
            else:
                one = pltpu.roll(one, 64, 1)
            tile = products_ref[1 - core, x, :, z * 64:z * 64 + 128] + jnp.where(left, one, two)
            logits_ref[0:entries, j * 128:(j + 1) * 128] = tile
            peak = jnp.max(tile, axis=0, keepdims=True)
            exponent = jnp.exp(tile - peak)
            hit = rows == targets_ref[j:j + 1, :] - first
            stats_ref[j:j + 1, :] = peak
            stats_ref[8 + j:9 + j, :] = jnp.sum(exponent, axis=0, keepdims=True)
            stats_ref[16 + j:17 + j, :] = jnp.sum(jnp.where(hit, exponent, 0.0), axis=0, keepdims=True)
        stats_ref[24:40, :] = floors_ref[...]

    return call(
        body,
        (
            jax.ShapeDtypeStruct((1024, 1024), jnp.float32),
            jax.ShapeDtypeStruct((40, 128), jnp.float32),
        ),
        "join_halves",
        (products, floor_stats, targets),
        vmem_mib=6,
        out_specs=(VMEM, VMEM),
    )


def join(axis, stats, before, last=None):
    size = SIZES[axis]
    hops = [0, 1] if size == 2 else [0, 1, 3, 2]
    pieces = [stats] + [shift(stats, axis, k) for k in hops[1:]]

    def body(*refs):
        piece_refs, rest = refs[:size], refs[size:]
        if before is not None:
            before_ref, rest = rest[0], rest[1:]
        held = rest[-1]
        mine = coordinate(axis)
        for piece_ref, k in zip(piece_refs, hops):
            held[lax.rem(mine - k + size, size)] = piece_ref[...]
        peak = held[0, 0:8]
        for i in range(1, size):
            peak = jnp.maximum(peak, held[i, 0:8])
        mass = target = floor = total = jnp.zeros((8, 128), jnp.float32)
        mass_before = total_before = jnp.zeros((8, 128), jnp.float32)
        if before is not None:
            mass_before = before_ref[0:8] * jnp.exp(piece_refs[0][0:8] - peak)
            total_before = before_ref[8:16]
        for i in range(size):
            scale = jnp.exp(held[i, 0:8] - peak)
            part = held[i, 8:16] * scale
            mass = mass + part
            target = target + held[i, 16:24] * scale
            floor = floor + held[i, 24:32]
            total = total + held[i, 32:40]
            earlier = i < mine
            mass_before = mass_before + jnp.where(earlier, part, 0.0)
            total_before = total_before + jnp.where(earlier, held[i, 32:40], 0.0)
        if last is None:
            stats_ref, after_ref = rest[0], rest[1]
            stats_ref[0:8] = peak
            stats_ref[8:16] = mass
            stats_ref[16:24] = target
            stats_ref[24:32] = floor
            stats_ref[32:40] = total
            after_ref[0:8] = mass_before
            after_ref[8:16] = total_before
        else:
            own_ref, totals_ref, terms_ref, bits_ref = rest[:4]
            tokens = totals_ref[...].astype(jnp.float32)
            free = (tokens - total) / mass
            terms_ref[0:8] = jnp.exp(own_ref[0:8] - peak) * free / tokens
            terms_ref[8:16] = 1.0 / tokens
            terms_ref[16:24] = (total_before + mass_before * free) / tokens
            bits_ref[...] = -jnp.log2((floor + target * free) / tokens)

    inputs = pieces + ([] if before is None else [before]) + ([] if last is None else list(last))
    first, second = ((40, 128), (16, 128)) if last is None else ((24, 128), (8, 128))
    return call(
        body,
        (jax.ShapeDtypeStruct(first, jnp.float32), jax.ShapeDtypeStruct(second, jnp.float32)),
        "join_" + axis,
        inputs,
        vmem_mib=2,
        scratch=[pltpu.VMEM((size, 40, 128), jnp.float32)],
        out_specs=(VMEM, VMEM),
    )


def finish(logits, floors, stats, terms, entries):
    block = 256

    def body(logits_ref, floors_ref, stats_ref, terms_ref, out_ref, carry_ref, floor_carry_ref):
        i = pl.program_id(0)

        @pl.when(i == 0)
        def _():
            carry_ref[...] = jnp.zeros_like(carry_ref)
            floor_carry_ref[...] = jnp.zeros_like(floor_carry_ref)

        rows = pl.ds(pl.multiple_of(i * block, block), block)
        below = lax.broadcasted_iota(jnp.int32, (block, block), 1)
        lower = (below < lax.broadcasted_iota(jnp.int32, (block, block), 0)).astype(jnp.bfloat16)
        floors = floors_ref[rows, :]
        floor_sums = floor_carry_ref[0:1, :] + jnp.dot(
            lower, floors.astype(jnp.bfloat16), preferred_element_type=jnp.float32
        )
        floor_carry_ref[0:1, :] += jnp.sum(floors, axis=0, keepdims=True)
        for j in range(0, ROWS, 2):
            lanes = slice(j * 128, (j + 2) * 128)
            peak, scale, inverse, offset = (
                jnp.concatenate([ref[at + j:at + j + 1, :], ref[at + j + 1:at + j + 2, :]], axis=1)
                for ref, at in ((stats_ref, 0), (terms_ref, 0), (terms_ref, 8), (terms_ref, 16))
            )
            value = jnp.exp(logits_ref[rows, lanes] - peak)
            high = value.astype(jnp.bfloat16)
            low = (value - high.astype(jnp.float32)).astype(jnp.bfloat16)
            sums = jnp.dot(lower, high, preferred_element_type=jnp.float32)
            sums = sums + jnp.dot(lower, low, preferred_element_type=jnp.float32)
            sums = sums + carry_ref[0:1, lanes]
            carry_ref[0:1, lanes] += jnp.sum(value, axis=0, keepdims=True)
            wide = jnp.concatenate([floor_sums, floor_sums], axis=1)
            out_ref[:, lanes] = sums * scale + wide * inverse + offset

    return call(
        body,
        jax.ShapeDtypeStruct((entries, 1024), jnp.float32),
        "finish",
        (logits, floors, stats, terms),
        vmem_mib=8,
        grid=(-(-entries // block),),
        scratch=[pltpu.VMEM((8, 1024), jnp.float32), pltpu.VMEM((8, 128), jnp.float32)],
        out_specs=pl.BlockSpec((block, 1024), lambda i: (i, 0)),
    )


def own_coordinate(axes):
    core = lax.rem(lax.axis_index(TENSOR), 2)
    return jnp.where(core == 0, coordinate(axes[0]), coordinate(axes[1]))


def square_sums(pieces):
    def body(*refs):
        mine = coordinate("y")
        total = jnp.zeros((64, 1), jnp.float32)
        for i, k in enumerate((0, 1, 3, 2)):
            piece = refs[i][...]
            place = lax.rem(mine - k + 4, 4)
            refs[4][:, pl.ds(pl.multiple_of(place * 1024, 1024), 1024)] = piece
            widened = piece.astype(jnp.float32)
            total = total + jnp.sum(widened * widened, axis=1, keepdims=True)
        refs[5][...] = jnp.broadcast_to(total, (64, 128))

    return call(
        body,
        (jax.ShapeDtypeStruct((64, 4096), jnp.bfloat16), jax.ShapeDtypeStruct((64, 128), jnp.float32)),
        "square_sums",
        pieces,
        vmem_mib=4,
        out_specs=(VMEM, VMEM),
    )


def normalize(features, own, other, gain):
    def body(features_ref, own_ref, other_ref, gain_ref, upper_ref, lower_ref):
        core = lax.rem(lax.axis_index(TENSOR), 2)
        mean_square = (own_ref[:, 0:1] + other_ref[:, 0:1]) * (1.0 / 8192)
        scale = lax.rsqrt(mean_square + epsilon)
        for y in range(4):
            lanes = slice(y * 1024, (y + 1) * 1024)
            row = gain_ref[:, pl.ds(pl.multiple_of((y * 2 + core) * 1024, 1024), 1024)]
            value = (features_ref[:, lanes].astype(jnp.float32) * scale * row).astype(jnp.bfloat16)
            upper_ref[:, lanes] = value[:32]
            lower_ref[:, lanes] = value[32:]

    shape = jax.ShapeDtypeStruct((32, 4096), jnp.bfloat16)
    return call(
        body,
        (shape, shape),
        "normalize",
        (features, own, other, gain),
        vmem_mib=4,
        out_specs=(VMEM, VMEM),
    )


def stack(pieces, axes):
    rows = 2 * pieces[0][2].shape[0]
    half = rows // 2

    def body(*refs):
        mine = own_coordinate(axes)
        for (side, hops, _), ref in zip(pieces, refs):
            place = lax.rem(mine + (4 - hops), 4)
            for i, out_ref in enumerate(refs[-2:]):

                @pl.when(place // 2 == i)
                def _():
                    at = pl.multiple_of((place - 2 * i) * rows + side * half, half)
                    out_ref[pl.ds(at, half), :] = ref[...]

    shape = jax.ShapeDtypeStruct((2 * rows, 4096), jnp.bfloat16)
    return call(
        body,
        (shape, shape),
        "stack",
        [piece[2] for piece in pieces],
        vmem_mib=4,
        out_specs=(VMEM, VMEM),
    )


def multiply(weight, products, pieces, side, axes):
    entries = weight.shape[0]
    arrays = [pieces[0][0]] if pieces[0][0] is pieces[1][0] else [piece[0] for piece in pieces]
    inputs = [weight] + ([] if products is None else [products]) + arrays

    def body(*refs):
        weight_ref, out_ref = refs[0], refs[-1]
        token_refs = refs[len(inputs) - len(arrays):len(inputs)]
        core = lax.rem(lax.axis_index(TENSOR), 2)
        features = core if side == 0 else 1 - core
        mine = coordinate_of(features, axes)
        total = None
        for y in range(4):
            far = pl.ds(pl.multiple_of((y * 2 + features) * 1024, 1024), 1024)
            value = [ref[:, y * 1024:(y + 1) * 1024] for ref in token_refs]
            value = value[0] if len(value) == 1 else jnp.concatenate(value, axis=0)
            product = lax.dot_general(
                weight_ref[:, far], value, (((1,), (1,)), ((), ())), preferred_element_type=jnp.float32
            )
            total = product if total is None else total + product
        for i, (_, hops, half) in enumerate(pieces):
            place = lax.rem(mine + (4 - hops), 4)
            out_ref[side, place, :, half * 128:half * 128 + 128] = total[:, i * 128:i * 128 + 128]

    return call(
        body,
        jax.ShapeDtypeStruct((2, 4, entries, 256), jnp.float32),
        "multiply",
        inputs,
        vmem_mib=6,
        input_output_aliases={} if products is None else {1: 0},
        cost_estimate=pl.CostEstimate(flops=2 * entries * 4096 * 256, bytes_accessed=4 << 20, transcendentals=0),
    )


def coordinate_of(core, axes):
    return jnp.where(core == 0, coordinate(axes[0]), coordinate(axes[1]))


def local(hidden, norm_gain, head_weight, floor_counts, totals, targets):
    weight = head_weight.T
    entries = weight.shape[0]
    targets = targets.reshape(8, 128)

    beside = [shift(hidden, "y", k) for k in (1, 3, 2)]
    floors, gain, floor_stats = prepare(floor_counts.reshape(1, entries), norm_gain, targets)
    raw, own = square_sums([hidden] + beside)
    upper, lower = normalize(raw, own, shift(own, "c", 1), gain)
    axes = "xz"
    upper_1, lower_3 = shift(upper, axes, 1), shift(lower, axes, 3)
    upper_3, lower_1 = shift(upper, axes, 3), shift(lower, axes, 1)
    upper_2, lower_2 = shift(upper_1, axes, 1), shift(lower_3, axes, 3)
    pieces = [(0, 0, upper), (1, 0, lower), (0, 1, upper_1), (1, 3, lower_3)]
    pieces += [(0, 3, upper_3), (1, 1, lower_1), (0, 2, upper_2), (1, 2, lower_2)]
    block = stack(pieces, axes)

    axes = "zx"
    swap = lambda value: shift(value, "c", 1)
    up = lambda value: shift(value, axes, 1)
    down = lambda value: shift(value, axes, 3)
    upper, lower = block
    upper_1, lower_3 = up(upper), down(lower)
    swapped = swap(upper), swap(lower)
    products = multiply(weight, None, [(upper, 0, 0), (lower, 0, 1)], 0, axes)
    upper, lower, products = lax.optimization_barrier((upper, lower, products))
    upper_3, lower_1 = down(upper), up(lower)
    products = multiply(weight, products, [(swapped[0], 0, 0), (swapped[1], 0, 1)], 1, axes)
    upper_1, lower_3, products = lax.optimization_barrier((upper_1, lower_3, products))
    upper_2, lower_2 = up(upper_1), down(lower_3)
    swapped = swap(upper_1), swap(lower_3)
    products = multiply(weight, products, [(upper_1, 1, 0), (lower_3, 3, 1)], 0, axes)
    products = multiply(weight, products, [(swapped[0], 1, 0), (swapped[1], 3, 1)], 1, axes)
    upper_3, lower_1, products = lax.optimization_barrier((upper_3, lower_1, products))
    swapped = swap(upper_3), swap(lower_1)
    products = multiply(weight, products, [(upper_3, 3, 0), (lower_1, 1, 1)], 0, axes)
    products = multiply(weight, products, [(swapped[0], 3, 0), (swapped[1], 1, 1)], 1, axes)
    upper_2, lower_2, products = lax.optimization_barrier((upper_2, lower_2, products))
    swapped = swap(upper_2), swap(lower_2)
    products = multiply(weight, products, [(upper_2, 2, 0), (lower_2, 2, 1)], 0, axes)
    products = multiply(weight, products, [(swapped[0], 2, 0), (swapped[1], 2, 1)], 1, axes)

    logits, stats = join_halves(products, floor_stats, targets)
    group, before = stats, None
    for axis in ("c", "y", "z"):
        group, before = join(axis, group, before)
    terms, bits = join("x", group, before, last=(stats, totals.reshape(8, 128)))
    cumulative = finish(logits, floors, stats, terms, entries)
    return cumulative.T, bits.reshape(1024)


def solution(mesh):
    in_specs = (P(STREAM, TENSOR), P(), P(None, BOTH), P(BOTH), P(), P())
    out_specs = (P(None, BOTH), P())
    return jax.shard_map(local, mesh=mesh, in_specs=in_specs, out_specs=out_specs, check_vma=False)
```

```python
import jax
import jax.numpy as jnp
from jax import lax
from jax.experimental import pallas as pl
from jax.experimental.pallas import tpu as pltpu
from jax.sharding import PartitionSpec as P

epsilon = 1e-05
STREAM, TENSOR = "stream", "tensor"
BOTH = (STREAM, TENSOR)
SIZES = {"x": 4, "z": 4, "y": 4, "c": 2}
STRIDES = {"x": 32, "z": 8, "y": 2, "c": 1}
ROWS = 8
VMEM = pl.BlockSpec(memory_space=pltpu.VMEM)


def coordinate(axis):
    index = lax.axis_index(STREAM) * 8 + lax.axis_index(TENSOR)
    return lax.rem(lax.div(index, STRIDES[axis]), SIZES[axis])


def shift(value, axis, hops):
    pairs = []
    for source in range(128):
        name = axis[source % len(axis)]
        size, stride = SIZES[name], STRIDES[name]
        place = source // stride % size
        pairs.append((source, source + ((place + hops) % size - place) * stride))
    return lax.ppermute(value, BOTH, pairs)


def call(body, out_shape, name, inputs, vmem_mib=32, scratch=(), out_specs=VMEM, **rest):
    return pl.pallas_call(
        body,
        out_shape=out_shape,
        in_specs=[VMEM] * len(inputs),
        out_specs=out_specs,
        scratch_shapes=list(scratch),
        compiler_params=pltpu.CompilerParams(vmem_limit_bytes=vmem_mib << 20),
        name=name,
        **rest,
    )(*inputs)


def prepare(weight, hidden, floor_counts, gain, targets):
    entries = weight.shape[0]

    def body(weight_hbm, hidden_hbm, floors_hbm, gain_hbm, targets_hbm,
             weight_ref, hidden_ref, columns_ref, gain_out_ref, stats_ref,
             row, floors_ref, gain_ref, targets_ref, sems):
        copies = [
            pltpu.make_async_copy(source, target, sems.at[i])
            for i, (source, target) in enumerate((
                (floors_hbm, floors_ref),
                (targets_hbm, targets_ref),
                (gain_hbm, gain_ref),
                (hidden_hbm, hidden_ref),
                (weight_hbm, weight_ref),
            ))
        ]
        for copy in copies:
            copy.start()
        for copy in copies[:3]:
            copy.wait()
        row[...] = jnp.zeros_like(row)
        row[:, 0:entries] = jnp.broadcast_to(floors_ref[...].astype(jnp.float32), (8, entries))
        total = jnp.zeros((1, 128), jnp.float32)
        picked = [jnp.zeros((1, 128), jnp.float32)] * ROWS
        for b in range(ROWS):
            columns = jnp.transpose(jnp.concatenate([row[:, b * 128:(b + 1) * 128]] * 16, axis=0))
            columns_ref[b * 128:(b + 1) * 128, :] = columns
            total = total + jnp.sum(columns, axis=0, keepdims=True)
            rows = lax.broadcasted_iota(jnp.int32, (128, 128), 0) + (b * 128 + first_entry(entries))
            for j in range(ROWS):
                hit = jnp.where(rows == targets_ref[j:j + 1, :], columns, 0.0)
                picked[j] = picked[j] + jnp.sum(hit, axis=0, keepdims=True)
        stats_ref[0:8] = jnp.concatenate(picked, axis=0)
        stats_ref[8:16] = jnp.broadcast_to(total, (8, 128))
        gain_out_ref[...] = gain_ref[...].astype(jnp.float32).reshape(1, 8192)
        for copy in copies[3:]:
            copy.wait()

    anywhere = pl.BlockSpec(memory_space=pltpu.HBM)
    operands = (weight, hidden, floor_counts, gain, targets)
    return pl.pallas_call(
        body,
        out_shape=(
            pltpu.VMEM(weight.shape, jnp.bfloat16),
            pltpu.VMEM(hidden.shape, jnp.bfloat16),
            pltpu.VMEM((1024, 128), jnp.float32),
            pltpu.VMEM((1, 8192), jnp.float32),
            pltpu.VMEM((16, 128), jnp.float32),
        ),
        in_specs=[anywhere] * 5,
        out_specs=(VMEM,) * 5,
        scratch_shapes=[
            pltpu.VMEM((8, 1024), jnp.float32),
            pltpu.VMEM((1, entries), jnp.int32),
            pltpu.VMEM((8192,), jnp.bfloat16),
            pltpu.VMEM((8, 128), jnp.int32),
            pltpu.SemaphoreType.DMA((5,)),
        ],
        compiler_params=pltpu.CompilerParams(vmem_limit_bytes=2 << 20),
        name="prepare",
    )(*(pltpu.with_memory_space_constraint(operand, pltpu.HBM) for operand in operands))


def first_entry(entries):
    return (lax.axis_index(STREAM) * 8 + lax.axis_index(TENSOR)) * entries


def join_halves(products, floor_stats, targets):
    entries = products.shape[2]

    def body(products_ref, floors_ref, targets_ref, logits_ref, stats_ref):
        core = lax.rem(lax.axis_index(TENSOR), 2)
        first = first_entry(entries)
        rows = lax.broadcasted_iota(jnp.int32, (entries, 128), 0)
        left = lax.broadcasted_iota(jnp.int32, (entries, 128), 1) < 64
        logits_ref[1000:1024, :] = jnp.full((24, 1024), -jnp.inf, jnp.float32)
        for j in range(ROWS):
            x, z = j // 2, j % 2 * 2
            near = slice(x // 2 * 128, x // 2 * 128 + 128)
            one, two = products_ref[core, z, :, near], products_ref[core, z + 1, :, near]
            if x % 2 == 0:
                two = pltpu.roll(two, 64, 1)
            else:
                one = pltpu.roll(one, 64, 1)
            tile = products_ref[1 - core, x, :, z * 64:z * 64 + 128] + jnp.where(left, one, two)
            logits_ref[0:entries, j * 128:(j + 1) * 128] = tile
            peak = jnp.max(tile, axis=0, keepdims=True)
            exponent = jnp.exp(tile - peak)
            hit = rows == targets_ref[j:j + 1, :] - first
            stats_ref[j:j + 1, :] = peak
            stats_ref[8 + j:9 + j, :] = jnp.sum(exponent, axis=0, keepdims=True)
            stats_ref[16 + j:17 + j, :] = jnp.sum(jnp.where(hit, exponent, 0.0), axis=0, keepdims=True)
        stats_ref[24:40, :] = floors_ref[...]

    return call(
        body,
        (
            jax.ShapeDtypeStruct((1024, 1024), jnp.float32),
            jax.ShapeDtypeStruct((40, 128), jnp.float32),
        ),
        "join_halves",
        (products, floor_stats, targets),
        vmem_mib=6,
        out_specs=(VMEM, VMEM),
    )


def join(axis, stats, before, last=None):
    size = SIZES[axis]
    hops = [0, 1] if size == 2 else [0, 1, 3, 2]
    pieces = [stats] + [shift(stats, axis, k) for k in hops[1:]]

    def body(*refs):
        piece_refs, rest = refs[:size], refs[size:]
        if before is not None:
            before_ref, rest = rest[0], rest[1:]
        held = rest[-1]
        mine = coordinate(axis)
        for piece_ref, k in zip(piece_refs, hops):
            held[lax.rem(mine - k + size, size)] = piece_ref[...]
        peak = held[0, 0:8]
        for i in range(1, size):
            peak = jnp.maximum(peak, held[i, 0:8])
        mass = target = floor = total = jnp.zeros((8, 128), jnp.float32)
        mass_before = total_before = jnp.zeros((8, 128), jnp.float32)
        if before is not None:
            mass_before = before_ref[0:8] * jnp.exp(piece_refs[0][0:8] - peak)
            total_before = before_ref[8:16]
        for i in range(size):
            scale = jnp.exp(held[i, 0:8] - peak)
            part = held[i, 8:16] * scale
            mass = mass + part
            target = target + held[i, 16:24] * scale
            floor = floor + held[i, 24:32]
            total = total + held[i, 32:40]
            earlier = i < mine
            mass_before = mass_before + jnp.where(earlier, part, 0.0)
            total_before = total_before + jnp.where(earlier, held[i, 32:40], 0.0)
        if last is None:
            stats_ref, after_ref = rest[0], rest[1]
            stats_ref[0:8] = peak
            stats_ref[8:16] = mass
            stats_ref[16:24] = target
            stats_ref[24:32] = floor
            stats_ref[32:40] = total
            after_ref[0:8] = mass_before
            after_ref[8:16] = total_before
        else:
            own_ref, totals_ref, terms_ref, bits_ref = rest[:4]
            tokens = totals_ref[...].astype(jnp.float32)
            free = (tokens - total) / mass
            terms_ref[0:8] = jnp.exp(own_ref[0:8] - peak) * free / tokens
            terms_ref[8:16] = 1.0 / tokens
            terms_ref[16:24] = (total_before + mass_before * free) / tokens
            bits_ref[...] = -jnp.log2((floor + target * free) / tokens)

    inputs = pieces + ([] if before is None else [before]) + ([] if last is None else list(last))
    first, second = ((40, 128), (16, 128)) if last is None else ((24, 128), (8, 128))
    return call(
        body,
        (jax.ShapeDtypeStruct(first, jnp.float32), jax.ShapeDtypeStruct(second, jnp.float32)),
        "join_" + axis,
        inputs,
        vmem_mib=2,
        scratch=[pltpu.VMEM((size, 40, 128), jnp.float32)],
        out_specs=(VMEM, VMEM),
    )


def finish(logits, floors, stats, terms, entries):
    block = 256

    def body(logits_ref, floors_ref, stats_ref, terms_ref, out_ref, carry_ref, floor_carry_ref):
        i = pl.program_id(0)

        @pl.when(i == 0)
        def _():
            carry_ref[...] = jnp.zeros_like(carry_ref)
            floor_carry_ref[...] = jnp.zeros_like(floor_carry_ref)

        rows = pl.ds(pl.multiple_of(i * block, block), block)
        below = lax.broadcasted_iota(jnp.int32, (block, block), 1)
        lower = (below < lax.broadcasted_iota(jnp.int32, (block, block), 0)).astype(jnp.bfloat16)
        floors = floors_ref[rows, :]
        floor_sums = floor_carry_ref[0:1, :] + jnp.dot(
            lower, floors.astype(jnp.bfloat16), preferred_element_type=jnp.float32
        )
        floor_carry_ref[0:1, :] += jnp.sum(floors, axis=0, keepdims=True)
        for j in range(0, ROWS, 2):
            lanes = slice(j * 128, (j + 2) * 128)
            peak, scale, inverse, offset = (
                jnp.concatenate([ref[at + j:at + j + 1, :], ref[at + j + 1:at + j + 2, :]], axis=1)
                for ref, at in ((stats_ref, 0), (terms_ref, 0), (terms_ref, 8), (terms_ref, 16))
            )
            value = jnp.exp(logits_ref[rows, lanes] - peak)
            high = value.astype(jnp.bfloat16)
            low = (value - high.astype(jnp.float32)).astype(jnp.bfloat16)
            sums = jnp.dot(lower, high, preferred_element_type=jnp.float32)
            sums = sums + jnp.dot(lower, low, preferred_element_type=jnp.float32)
            sums = sums + carry_ref[0:1, lanes]
            carry_ref[0:1, lanes] += jnp.sum(value, axis=0, keepdims=True)
            wide = jnp.concatenate([floor_sums, floor_sums], axis=1)
            out_ref[:, lanes] = sums * scale + wide * inverse + offset

    return call(
        body,
        jax.ShapeDtypeStruct((entries, 1024), jnp.float32),
        "finish",
        (logits, floors, stats, terms),
        vmem_mib=8,
        grid=(-(-entries // block),),
        scratch=[pltpu.VMEM((8, 1024), jnp.float32), pltpu.VMEM((8, 128), jnp.float32)],
        out_specs=pl.BlockSpec((block, 1024), lambda i: (i, 0)),
    )


def own_coordinate(axes):
    core = lax.rem(lax.axis_index(TENSOR), 2)
    return jnp.where(core == 0, coordinate(axes[0]), coordinate(axes[1]))


def square_sums(pieces):
    def body(*refs):
        mine = coordinate("y")
        total = jnp.zeros((64, 1), jnp.float32)
        for i, k in enumerate((0, 1, 3, 2)):
            piece = refs[i][...]
            place = lax.rem(mine - k + 4, 4)
            refs[4][:, pl.ds(pl.multiple_of(place * 1024, 1024), 1024)] = piece
            widened = piece.astype(jnp.float32)
            total = total + jnp.sum(widened * widened, axis=1, keepdims=True)
        refs[5][...] = jnp.broadcast_to(total, (64, 128))

    return call(
        body,
        (jax.ShapeDtypeStruct((64, 4096), jnp.bfloat16), jax.ShapeDtypeStruct((64, 128), jnp.float32)),
        "square_sums",
        pieces,
        vmem_mib=4,
        out_specs=(VMEM, VMEM),
    )


def normalize(features, own, other, gain):
    def body(features_ref, own_ref, other_ref, gain_ref, upper_ref, lower_ref):
        core = lax.rem(lax.axis_index(TENSOR), 2)
        mean_square = (own_ref[:, 0:1] + other_ref[:, 0:1]) * (1.0 / 8192)
        scale = lax.rsqrt(mean_square + epsilon)
        for y in range(4):
            lanes = slice(y * 1024, (y + 1) * 1024)
            row = gain_ref[:, pl.ds(pl.multiple_of((y * 2 + core) * 1024, 1024), 1024)]
            value = (features_ref[:, lanes].astype(jnp.float32) * scale * row).astype(jnp.bfloat16)
            upper_ref[:, lanes] = value[:32]
            lower_ref[:, lanes] = value[32:]

    shape = jax.ShapeDtypeStruct((32, 4096), jnp.bfloat16)
    return call(
        body,
        (shape, shape),
        "normalize",
        (features, own, other, gain),
        vmem_mib=4,
        out_specs=(VMEM, VMEM),
    )


def stack(pieces, axes):
    rows = 2 * pieces[0][2].shape[0]
    half = rows // 2

    def body(*refs):
        mine = own_coordinate(axes)
        for (side, hops, _), ref in zip(pieces, refs):
            place = lax.rem(mine + (4 - hops), 4)
            for i, out_ref in enumerate(refs[-2:]):

                @pl.when(place // 2 == i)
                def _():
                    at = pl.multiple_of((place - 2 * i) * rows + side * half, half)
                    out_ref[pl.ds(at, half), :] = ref[...]

    shape = jax.ShapeDtypeStruct((2 * rows, 4096), jnp.bfloat16)
    return call(
        body,
        (shape, shape),
        "stack",
        [piece[2] for piece in pieces],
        vmem_mib=4,
        out_specs=(VMEM, VMEM),
    )


def multiply(weight, products, pieces, side, axes, keep=False):
    entries = weight.shape[0]
    arrays = [pieces[0][0]] if pieces[0][0] is pieces[1][0] else [piece[0] for piece in pieces]
    inputs = [weight] + ([] if products is None else [products]) + arrays

    def body(*refs):
        weight_ref, out_ref = refs[0], refs[len(inputs)]
        token_refs = refs[len(inputs) - len(arrays):len(inputs)]
        core = lax.rem(lax.axis_index(TENSOR), 2)
        features = core if side == 0 else 1 - core
        mine = coordinate_of(features, axes)
        total = None
        for y in range(4):
            far = pl.ds(pl.multiple_of((y * 2 + features) * 1024, 1024), 1024)
            value = [ref[:, y * 1024:(y + 1) * 1024] for ref in token_refs]
            value = value[0] if len(value) == 1 else jnp.concatenate(value, axis=0)
            if keep:
                refs[-1][:, y * 1024:(y + 1) * 1024] = value
            product = lax.dot_general(
                weight_ref[:, far], value, (((1,), (1,)), ((), ())), preferred_element_type=jnp.float32
            )
            total = product if total is None else total + product
        for i, (_, hops, half) in enumerate(pieces):
            place = lax.rem(mine + (4 - hops), 4)
            out_ref[side, place, :, half * 128:half * 128 + 128] = total[:, i * 128:i * 128 + 128]

    shape = jax.ShapeDtypeStruct((2, 4, entries, 256), jnp.float32)
    return call(
        body,
        (shape, jax.ShapeDtypeStruct((256, 4096), jnp.bfloat16)) if keep else shape,
        "multiply",
        inputs,
        vmem_mib=6,
        out_specs=(VMEM, VMEM) if keep else VMEM,
        input_output_aliases={} if products is None else {1: 0},
        cost_estimate=pl.CostEstimate(flops=2 * entries * 4096 * 256, bytes_accessed=4 << 20, transcendentals=0),
    )


def coordinate_of(core, axes):
    return jnp.where(core == 0, coordinate(axes[0]), coordinate(axes[1]))


def local(hidden, norm_gain, head_weight, floor_counts, totals, targets):
    weight = head_weight.T
    entries = weight.shape[0]
    targets = targets.reshape(8, 128)

    beside = [shift(hidden, "y", k) for k in (1, 3, 2)]
    weight, hidden, floors, gain, floor_stats = prepare(
        weight, hidden, floor_counts.reshape(1, entries), norm_gain, targets
    )
    weight, *beside = lax.optimization_barrier((weight, *beside))
    raw, own = square_sums([hidden] + beside)
    upper, lower = normalize(raw, own, shift(own, "c", 1), gain)
    axes = "xz"
    upper_1, lower_3 = shift(upper, axes, 1), shift(lower, axes, 3)
    upper_3, lower_1 = shift(upper, axes, 3), shift(lower, axes, 1)
    upper_2, lower_2 = shift(upper_1, axes, 1), shift(lower_3, axes, 3)
    pieces = [(0, 0, upper), (1, 0, lower), (0, 1, upper_1), (1, 3, lower_3)]
    pieces += [(0, 3, upper_3), (1, 1, lower_1), (0, 2, upper_2), (1, 2, lower_2)]
    block = stack(pieces, axes)

    axes = "zx"
    swap = lambda value: shift(value, "c", 1)
    up = lambda value: shift(value, axes, 1)
    down = lambda value: shift(value, axes, 3)
    upper, lower = block
    hold = lax.optimization_barrier
    upper_1, lower_3 = up(upper), down(lower)
    swapped = swap(upper), swap(lower)
    products = multiply(weight, None, [(upper, 0, 0), (lower, 0, 1)], 0, axes)
    upper, lower, products = hold((upper, lower, products))
    upper_3, lower_1 = down(upper), up(lower)
    products = multiply(weight, products, [(swapped[0], 0, 0), (swapped[1], 0, 1)], 1, axes)
    upper_1, lower_3, products = hold((upper_1, lower_3, products))
    upper_2, lower_2 = up(upper_1), down(lower_3)
    swapped_1 = swap(upper_1), swap(lower_3)
    products = multiply(weight, products, [(upper_1, 1, 0), (lower_3, 3, 1)], 0, axes)
    products = multiply(weight, products, [(upper_3, 3, 0), (lower_1, 1, 1)], 0, axes)
    upper_2, lower_2, upper_3, lower_1, products = hold((upper_2, lower_2, upper_3, lower_1, products))
    swapped_3 = swap(upper_3), swap(lower_1)
    swapped_2 = swap(upper_2), swap(lower_2)
    products = multiply(weight, products, [(upper_2, 2, 0), (lower_2, 2, 1)], 0, axes)
    products = multiply(weight, products, [(swapped_1[0], 1, 0), (swapped_1[1], 3, 1)], 1, axes)
    products = multiply(weight, products, [(swapped_3[0], 3, 0), (swapped_3[1], 1, 1)], 1, axes)
    products = multiply(weight, products, [(swapped_2[0], 2, 0), (swapped_2[1], 2, 1)], 1, axes)

    logits, stats = join_halves(products, floor_stats, targets)
    group, before = stats, None
    for axis in ("c", "y", "z"):
        group, before = join(axis, group, before)
    terms, bits = join("x", group, before, last=(stats, totals.reshape(8, 128)))
    cumulative = finish(logits, floors, stats, terms, entries)
    return cumulative.T, bits.reshape(1024)


def solution(mesh):
    in_specs = (P(STREAM, TENSOR), P(), P(None, BOTH), P(BOTH), P(), P())
    out_specs = (P(None, BOTH), P())
    return jax.shard_map(local, mesh=mesh, in_specs=in_specs, out_specs=out_specs, check_vma=False)
```

```python
import jax
import jax.numpy as jnp
from jax import lax
from jax.experimental import pallas as pl
from jax.experimental.pallas import tpu as pltpu
from jax.sharding import PartitionSpec as P

epsilon = 1e-05
STREAM, TENSOR = "stream", "tensor"
BOTH = (STREAM, TENSOR)
SIZES = {"x": 4, "z": 4, "y": 4, "c": 2}
STRIDES = {"x": 32, "z": 8, "y": 2, "c": 1}
ROWS = 8
VMEM = pl.BlockSpec(memory_space=pltpu.VMEM)


def coordinate(axis):
    index = lax.axis_index(STREAM) * 8 + lax.axis_index(TENSOR)
    return lax.rem(lax.div(index, STRIDES[axis]), SIZES[axis])


def shift(value, axis, hops):
    pairs = []
    for source in range(128):
        name = axis[source % len(axis)]
        size, stride = SIZES[name], STRIDES[name]
        place = source // stride % size
        pairs.append((source, source + ((place + hops) % size - place) * stride))
    return lax.ppermute(value, BOTH, pairs)


def call(body, out_shape, name, inputs, vmem_mib=32, scratch=(), out_specs=VMEM, **rest):
    return pl.pallas_call(
        body,
        out_shape=out_shape,
        in_specs=[VMEM] * len(inputs),
        out_specs=out_specs,
        scratch_shapes=list(scratch),
        compiler_params=pltpu.CompilerParams(vmem_limit_bytes=vmem_mib << 20),
        name=name,
        **rest,
    )(*inputs)


def prepare(weight, hidden, floor_counts, gain, targets):
    entries = weight.shape[0]

    def body(weight_hbm, hidden_hbm, floors_hbm, gain_hbm, targets_hbm,
             weight_ref, hidden_ref, columns_ref, gain_out_ref, stats_ref,
             row, floors_ref, gain_ref, targets_ref, sems):
        copies = [
            pltpu.make_async_copy(source, target, sems.at[i])
            for i, (source, target) in enumerate((
                (floors_hbm, floors_ref),
                (targets_hbm, targets_ref),
                (gain_hbm, gain_ref),
                (hidden_hbm, hidden_ref),
                (weight_hbm, weight_ref),
            ))
        ]
        for copy in copies:
            copy.start()
        for copy in copies[:3]:
            copy.wait()
        row[...] = jnp.zeros_like(row)
        row[:, 0:entries] = jnp.broadcast_to(floors_ref[...].astype(jnp.float32), (8, entries))
        total = jnp.zeros((1, 128), jnp.float32)
        picked = [jnp.zeros((1, 128), jnp.float32)] * ROWS
        for b in range(ROWS):
            columns = jnp.transpose(jnp.concatenate([row[:, b * 128:(b + 1) * 128]] * 16, axis=0))
            columns_ref[b * 128:(b + 1) * 128, :] = columns
            total = total + jnp.sum(columns, axis=0, keepdims=True)
            rows = lax.broadcasted_iota(jnp.int32, (128, 128), 0) + (b * 128 + first_entry(entries))
            for j in range(ROWS):
                hit = jnp.where(rows == targets_ref[j:j + 1, :], columns, 0.0)
                picked[j] = picked[j] + jnp.sum(hit, axis=0, keepdims=True)
        stats_ref[0:8] = jnp.concatenate(picked, axis=0)
        stats_ref[8:16] = jnp.broadcast_to(total, (8, 128))
        gain_out_ref[...] = gain_ref[...].astype(jnp.float32).reshape(1, 8192)
        for copy in copies[3:]:
            copy.wait()

    anywhere = pl.BlockSpec(memory_space=pltpu.HBM)
    operands = (weight, hidden, floor_counts, gain, targets)
    return pl.pallas_call(
        body,
        out_shape=(
            pltpu.VMEM(weight.shape, jnp.bfloat16),
            pltpu.VMEM(hidden.shape, jnp.bfloat16),
            pltpu.VMEM((1024, 128), jnp.float32),
            pltpu.VMEM((1, 8192), jnp.float32),
            pltpu.VMEM((16, 128), jnp.float32),
        ),
        in_specs=[anywhere] * 5,
        out_specs=(VMEM,) * 5,
        scratch_shapes=[
            pltpu.VMEM((8, 1024), jnp.float32),
            pltpu.VMEM((1, entries), jnp.int32),
            pltpu.VMEM((8192,), jnp.bfloat16),
            pltpu.VMEM((8, 128), jnp.int32),
            pltpu.SemaphoreType.DMA((5,)),
        ],
        compiler_params=pltpu.CompilerParams(vmem_limit_bytes=2 << 20),
        name="prepare",
    )(*(pltpu.with_memory_space_constraint(operand, pltpu.HBM) for operand in operands))


def first_entry(entries):
    return (lax.axis_index(STREAM) * 8 + lax.axis_index(TENSOR)) * entries


def join_halves(products, floor_stats, targets):
    entries = products.shape[2]

    def body(products_ref, floors_ref, targets_ref, weights_ref, stats_ref):
        core = lax.rem(lax.axis_index(TENSOR), 2)
        first = first_entry(entries)
        rows = lax.broadcasted_iota(jnp.int32, (entries, 128), 0)
        left = lax.broadcasted_iota(jnp.int32, (entries, 128), 1) < 64
        weights_ref[1000:1024, :] = jnp.zeros((24, 1024), jnp.float32)
        for j in range(ROWS):
            x, z = j // 2, j % 2 * 2
            near = slice(x // 2 * 128, x // 2 * 128 + 128)
            one, two = products_ref[core, z, :, near], products_ref[core, z + 1, :, near]
            if x % 2 == 0:
                two = pltpu.roll(two, 64, 1)
            else:
                one = pltpu.roll(one, 64, 1)
            tile = products_ref[1 - core, x, :, z * 64:z * 64 + 128] + jnp.where(left, one, two)
            peak = jnp.max(tile, axis=0, keepdims=True)
            exponent = jnp.exp(tile - peak)
            weights_ref[0:entries, j * 128:(j + 1) * 128] = exponent
            hit = rows == targets_ref[j:j + 1, :] - first
            stats_ref[j:j + 1, :] = peak
            stats_ref[8 + j:9 + j, :] = jnp.sum(exponent, axis=0, keepdims=True)
            stats_ref[16 + j:17 + j, :] = jnp.sum(jnp.where(hit, exponent, 0.0), axis=0, keepdims=True)
        stats_ref[24:40, :] = floors_ref[...]

    return call(
        body,
        (
            jax.ShapeDtypeStruct((1024, 1024), jnp.float32),
            jax.ShapeDtypeStruct((40, 128), jnp.float32),
        ),
        "join_halves",
        (products, floor_stats, targets),
        vmem_mib=6,
        out_specs=(VMEM, VMEM),
    )


def join(axis, stats, before, last=None):
    size = SIZES[axis]
    hops = [0, 1] if size == 2 else [0, 1, 3, 2]
    pieces = [stats] + [shift(stats, axis, k) for k in hops[1:]]

    def body(*refs):
        piece_refs, rest = refs[:size], refs[size:]
        if before is not None:
            before_ref, rest = rest[0], rest[1:]
        held = rest[-1]
        mine = coordinate(axis)
        for piece_ref, k in zip(piece_refs, hops):
            held[lax.rem(mine - k + size, size)] = piece_ref[...]
        peak = held[0, 0:8]
        for i in range(1, size):
            peak = jnp.maximum(peak, held[i, 0:8])
        mass = target = floor = total = jnp.zeros((8, 128), jnp.float32)
        mass_before = total_before = jnp.zeros((8, 128), jnp.float32)
        if before is not None:
            mass_before = before_ref[0:8] * jnp.exp(piece_refs[0][0:8] - peak)
            total_before = before_ref[8:16]
        for i in range(size):
            scale = jnp.exp(held[i, 0:8] - peak)
            part = held[i, 8:16] * scale
            mass = mass + part
            target = target + held[i, 16:24] * scale
            floor = floor + held[i, 24:32]
            total = total + held[i, 32:40]
            earlier = i < mine
            mass_before = mass_before + jnp.where(earlier, part, 0.0)
            total_before = total_before + jnp.where(earlier, held[i, 32:40], 0.0)
        if last is None:
            stats_ref, after_ref = rest[0], rest[1]
            stats_ref[0:8] = peak
            stats_ref[8:16] = mass
            stats_ref[16:24] = target
            stats_ref[24:32] = floor
            stats_ref[32:40] = total
            after_ref[0:8] = mass_before
            after_ref[8:16] = total_before
        else:
            own_ref, totals_ref, terms_ref, bits_ref = rest[:4]
            tokens = totals_ref[...].astype(jnp.float32)
            free = (tokens - total) / mass
            terms_ref[0:8] = jnp.exp(own_ref[0:8] - peak) * free / tokens
            terms_ref[8:16] = 1.0 / tokens
            terms_ref[16:24] = (total_before + mass_before * free) / tokens
            bits_ref[...] = -jnp.log2((floor + target * free) / tokens)

    inputs = pieces + ([] if before is None else [before]) + ([] if last is None else list(last))
    first, second = ((40, 128), (16, 128)) if last is None else ((24, 128), (8, 128))
    return call(
        body,
        (jax.ShapeDtypeStruct(first, jnp.float32), jax.ShapeDtypeStruct(second, jnp.float32)),
        "join_" + axis,
        inputs,
        vmem_mib=2,
        scratch=[pltpu.VMEM((size, 40, 128), jnp.float32)],
        out_specs=(VMEM, VMEM),
    )


def running_sums(weights, floors):
    block = 256

    def body(weights_ref, floors_ref, sums_ref, floor_sums_ref):
        below = lax.broadcasted_iota(jnp.int32, (block, block), 1)
        lower = (below < lax.broadcasted_iota(jnp.int32, (block, block), 0)).astype(jnp.bfloat16)
        carry = [jnp.zeros((1, 256), jnp.float32)] * (ROWS // 2)
        floor_carry = jnp.zeros((1, 128), jnp.float32)
        for b in range(1024 // block):
            rows = slice(b * block, (b + 1) * block)
            floors = floors_ref[rows, :]
            floor_sums_ref[rows, :] = floor_carry + jnp.dot(
                lower, floors.astype(jnp.bfloat16), preferred_element_type=jnp.float32
            )
            floor_carry = floor_carry + jnp.sum(floors, axis=0, keepdims=True)
            for j in range(ROWS // 2):
                lanes = slice(j * 256, (j + 1) * 256)
                value = weights_ref[rows, lanes]
                high = value.astype(jnp.bfloat16)
                low = (value - high.astype(jnp.float32)).astype(jnp.bfloat16)
                sums = jnp.dot(lower, high, preferred_element_type=jnp.float32)
                sums = sums + jnp.dot(lower, low, preferred_element_type=jnp.float32)
                sums_ref[rows, lanes] = sums + carry[j]
                carry[j] = carry[j] + jnp.sum(value, axis=0, keepdims=True)

    return call(
        body,
        (
            jax.ShapeDtypeStruct((1024, 1024), jnp.float32),
            jax.ShapeDtypeStruct((1024, 128), jnp.float32),
        ),
        "running_sums",
        (weights, floors),
        vmem_mib=4,
        out_specs=(VMEM, VMEM),
    )


def finish(sums, floor_sums, terms, entries):
    def body(sums_ref, floors_ref, terms_ref, out_hbm, out_ref, sems):
        copies = []
        for j in range(ROWS):
            lanes = slice(j * 128, (j + 1) * 128)
            out_ref[:, lanes] = (
                sums_ref[0:entries, lanes] * terms_ref[j:j + 1, :]
                + floors_ref[0:entries, :] * terms_ref[8 + j:9 + j, :]
                + terms_ref[16 + j:17 + j, :]
            )
            copies.append(pltpu.make_async_copy(out_ref.at[:, lanes], out_hbm.at[:, lanes], sems.at[j]))
            copies[-1].start()
        for copy in copies:
            copy.wait()

    return call(
        body,
        jax.ShapeDtypeStruct((entries, 1024), jnp.float32),
        "finish",
        (sums, floor_sums, terms),
        vmem_mib=8,
        scratch=[pltpu.VMEM((entries, 1024), jnp.float32), pltpu.SemaphoreType.DMA((ROWS,))],
        out_specs=pl.BlockSpec(memory_space=pltpu.HBM),
    )


def own_coordinate(axes):
    core = lax.rem(lax.axis_index(TENSOR), 2)
    return jnp.where(core == 0, coordinate(axes[0]), coordinate(axes[1]))


def square_sums(pieces):
    def body(*refs):
        mine = coordinate("y")
        total = jnp.zeros((64, 1), jnp.float32)
        for i, k in enumerate((0, 1, 3, 2)):
            piece = refs[i][...]
            place = lax.rem(mine - k + 4, 4)
            refs[4][:, pl.ds(pl.multiple_of(place * 1024, 1024), 1024)] = piece
            widened = piece.astype(jnp.float32)
            total = total + jnp.sum(widened * widened, axis=1, keepdims=True)
        refs[5][...] = jnp.broadcast_to(total, (64, 128))

    return call(
        body,
        (jax.ShapeDtypeStruct((64, 4096), jnp.bfloat16), jax.ShapeDtypeStruct((64, 128), jnp.float32)),
        "square_sums",
        pieces,
        vmem_mib=4,
        out_specs=(VMEM, VMEM),
    )


def normalize(features, own, other, gain):
    def body(features_ref, own_ref, other_ref, gain_ref, upper_ref, lower_ref):
        core = lax.rem(lax.axis_index(TENSOR), 2)
        mean_square = (own_ref[:, 0:1] + other_ref[:, 0:1]) * (1.0 / 8192)
        scale = lax.rsqrt(mean_square + epsilon)
        for y in range(4):
            lanes = slice(y * 1024, (y + 1) * 1024)
            row = gain_ref[:, pl.ds(pl.multiple_of((y * 2 + core) * 1024, 1024), 1024)]
            value = (features_ref[:, lanes].astype(jnp.float32) * scale * row).astype(jnp.bfloat16)
            upper_ref[:, lanes] = value[:32]
            lower_ref[:, lanes] = value[32:]

    shape = jax.ShapeDtypeStruct((32, 4096), jnp.bfloat16)
    return call(
        body,
        (shape, shape),
        "normalize",
        (features, own, other, gain),
        vmem_mib=4,
        out_specs=(VMEM, VMEM),
    )


def stack(pieces, axes):
    rows = 2 * pieces[0][2].shape[0]
    half = rows // 2

    def body(*refs):
        mine = own_coordinate(axes)
        for (side, hops, _), ref in zip(pieces, refs):
            place = lax.rem(mine + (4 - hops), 4)
            refs[-3][pl.ds(pl.multiple_of(place * rows + side * half, half), half), :] = ref[...]
            for i, out_ref in enumerate(refs[-2:]):

                @pl.when(place // 2 == i)
                def _():
                    at = pl.multiple_of((place - 2 * i) * rows + side * half, half)
                    out_ref[pl.ds(at, half), :] = ref[...]

    whole = jax.ShapeDtypeStruct((4 * rows, 4096), jnp.bfloat16)
    shape = jax.ShapeDtypeStruct((2 * rows, 4096), jnp.bfloat16)
    return call(
        body,
        (whole, shape, shape),
        "stack",
        [piece[2] for piece in pieces],
        vmem_mib=4,
        out_specs=(VMEM, VMEM, VMEM),
    )


def multiply(weight, products, pieces, side, axes, keep=False):
    entries = weight.shape[0]
    arrays = [pieces[0][0]] if pieces[0][0] is pieces[1][0] else [piece[0] for piece in pieces]
    inputs = [weight] + ([] if products is None else [products]) + arrays

    def body(*refs):
        weight_ref, out_ref = refs[0], refs[len(inputs)]
        token_refs = refs[len(inputs) - len(arrays):len(inputs)]
        core = lax.rem(lax.axis_index(TENSOR), 2)
        features = core if side == 0 else 1 - core
        mine = coordinate_of(features, axes)
        total = None
        for y in range(4):
            far = pl.ds(pl.multiple_of((y * 2 + features) * 1024, 1024), 1024)
            value = [ref[:, y * 1024:(y + 1) * 1024] for ref in token_refs]
            value = value[0] if len(value) == 1 else jnp.concatenate(value, axis=0)
            if keep:
                refs[-1][:, y * 1024:(y + 1) * 1024] = value
            product = lax.dot_general(
                weight_ref[:, far], value, (((1,), (1,)), ((), ())), preferred_element_type=jnp.float32
            )
            total = product if total is None else total + product
        for i, (_, hops, half) in enumerate(pieces):
            place = lax.rem(mine + (4 - hops), 4)
            out_ref[side, place, :, half * 128:half * 128 + 128] = total[:, i * 128:i * 128 + 128]

    shape = jax.ShapeDtypeStruct((2, 4, entries, 256), jnp.float32)
    return call(
        body,
        (shape, jax.ShapeDtypeStruct((256, 4096), jnp.bfloat16)) if keep else shape,
        "multiply",
        inputs,
        vmem_mib=6,
        out_specs=(VMEM, VMEM) if keep else VMEM,
        input_output_aliases={} if products is None else {1: 0},
        cost_estimate=pl.CostEstimate(flops=2 * entries * 4096 * 256, bytes_accessed=4 << 20, transcendentals=0),
    )


def coordinate_of(core, axes):
    return jnp.where(core == 0, coordinate(axes[0]), coordinate(axes[1]))


def local(hidden, norm_gain, head_weight, floor_counts, totals, targets):
    weight = head_weight.T
    entries = weight.shape[0]
    targets = targets.reshape(8, 128)

    beside = [shift(hidden, "y", k) for k in (1, 3, 2)]
    weight, hidden, floors, gain, floor_stats = prepare(
        weight, hidden, floor_counts.reshape(1, entries), norm_gain, targets
    )
    weight, *beside = lax.optimization_barrier((weight, *beside))
    raw, own = square_sums([hidden] + beside)
    upper, lower = normalize(raw, own, shift(own, "c", 1), gain)
    axes = "xz"
    upper_1, lower_3 = shift(upper, axes, 1), shift(lower, axes, 3)
    upper_3, lower_1 = shift(upper, axes, 3), shift(lower, axes, 1)
    upper_2, lower_2 = shift(upper_1, axes, 1), shift(lower_3, axes, 3)
    pieces = [(0, 0, upper), (1, 0, lower), (0, 1, upper_1), (1, 3, lower_3)]
    pieces += [(0, 3, upper_3), (1, 1, lower_1), (0, 2, upper_2), (1, 2, lower_2)]
    block, upper, lower = stack(pieces, axes)

    axes = "zx"
    swap = lambda value: shift(value, "c", 1)
    up = lambda value: shift(value, axes, 1)
    down = lambda value: shift(value, axes, 3)
    hold = lax.optimization_barrier
    upper_1, lower_3 = up(upper), down(lower)
    swapped = swap(block)
    products = multiply(weight, None, [(block, 0, 0), (block, 0, 1)], 0, axes)
    upper, lower, products = hold((upper, lower, products))
    upper_3, lower_1 = down(upper), up(lower)
    products = multiply(weight, products, [(swapped, 0, 0), (swapped, 0, 1)], 1, axes)
    upper_1, lower_3, products = hold((upper_1, lower_3, products))
    upper_2, lower_2 = up(upper_1), down(lower_3)
    swapped_1 = swap(upper_1), swap(lower_3)
    products = multiply(weight, products, [(upper_1, 1, 0), (lower_3, 3, 1)], 0, axes)
    products = multiply(weight, products, [(upper_3, 3, 0), (lower_1, 1, 1)], 0, axes)
    upper_2, lower_2, upper_3, lower_1, products = hold((upper_2, lower_2, upper_3, lower_1, products))
    swapped_3 = swap(upper_3), swap(lower_1)
    swapped_2 = swap(upper_2), swap(lower_2)
    products = multiply(weight, products, [(upper_2, 2, 0), (lower_2, 2, 1)], 0, axes)
    products = multiply(weight, products, [(swapped_1[0], 1, 0), (swapped_1[1], 3, 1)], 1, axes)
    products = multiply(weight, products, [(swapped_3[0], 3, 0), (swapped_3[1], 1, 1)], 1, axes)
    products = multiply(weight, products, [(swapped_2[0], 2, 0), (swapped_2[1], 2, 1)], 1, axes)

    weights, stats = join_halves(products, floor_stats, targets)
    sums, floor_sums = running_sums(weights, floors)
    group, before = stats, None
    for axis in ("c", "y", "z"):
        group, before = join(axis, group, before)
    terms, bits = join("x", group, before, last=(stats, totals.reshape(8, 128)))
    cumulative = finish(sums, floor_sums, terms, entries)
    return cumulative.T, bits.reshape(1024)


def solution(mesh):
    in_specs = (P(STREAM, TENSOR), P(), P(None, BOTH), P(BOTH), P(), P())
    out_specs = (P(None, BOTH), P())
    return jax.shard_map(local, mesh=mesh, in_specs=in_specs, out_specs=out_specs, check_vma=False)
```

```python
import jax
import jax.numpy as jnp
from jax import lax
from jax.experimental import pallas as pl
from jax.experimental.pallas import tpu as pltpu
from jax.sharding import PartitionSpec as P

epsilon = 1e-05
STREAM, TENSOR = "stream", "tensor"
BOTH = (STREAM, TENSOR)
SIZES = {"x": 4, "z": 4, "y": 4, "c": 2}
STRIDES = {"x": 32, "z": 8, "y": 2, "c": 1}
ROWS = 8
VMEM = pl.BlockSpec(memory_space=pltpu.VMEM)


def coordinate(axis):
    index = lax.axis_index(STREAM) * 8 + lax.axis_index(TENSOR)
    return lax.rem(lax.div(index, STRIDES[axis]), SIZES[axis])


def shift(value, axis, hops, cross=False):
    pairs = []
    for source in range(128):
        name = axis[source % len(axis)]
        size, stride = SIZES[name], STRIDES[name]
        place = source // stride % size
        target = source + ((place + hops) % size - place) * stride
        pairs.append((source, target ^ 1 if cross else target))
    return lax.ppermute(value, BOTH, pairs)


def call(body, out_shape, name, inputs, vmem_mib=32, scratch=(), out_specs=VMEM, **rest):
    return pl.pallas_call(
        body,
        out_shape=out_shape,
        in_specs=[VMEM] * len(inputs),
        out_specs=out_specs,
        scratch_shapes=list(scratch),
        compiler_params=pltpu.CompilerParams(vmem_limit_bytes=vmem_mib << 20),
        name=name,
        **rest,
    )(*inputs)


def prepare(weight, hidden, floor_counts, gain, targets):
    entries = weight.shape[0]

    def body(weight_hbm, hidden_hbm, floors_hbm, gain_hbm, targets_hbm,
             weight_ref, hidden_ref, columns_ref, gain_out_ref, stats_ref,
             row, floors_ref, gain_ref, targets_ref, sems):
        copies = [
            pltpu.make_async_copy(source, target, sems.at[i])
            for i, (source, target) in enumerate((
                (floors_hbm, floors_ref),
                (targets_hbm, targets_ref),
                (gain_hbm, gain_ref),
                (hidden_hbm, hidden_ref),
                (weight_hbm, weight_ref),
            ))
        ]
        for copy in copies:
            copy.start()
        for copy in copies[:3]:
            copy.wait()
        row[...] = jnp.zeros_like(row)
        row[:, 0:entries] = jnp.broadcast_to(floors_ref[...].astype(jnp.float32), (8, entries))
        total = jnp.zeros((1, 128), jnp.float32)
        picked = [jnp.zeros((1, 128), jnp.float32)] * ROWS
        for b in range(ROWS):
            columns = jnp.transpose(jnp.concatenate([row[:, b * 128:(b + 1) * 128]] * 16, axis=0))
            columns_ref[b * 128:(b + 1) * 128, :] = columns
            total = total + jnp.sum(columns, axis=0, keepdims=True)
            rows = lax.broadcasted_iota(jnp.int32, (128, 128), 0) + (b * 128 + first_entry(entries))
            for j in range(ROWS):
                hit = jnp.where(rows == targets_ref[j:j + 1, :], columns, 0.0)
                picked[j] = picked[j] + jnp.sum(hit, axis=0, keepdims=True)
        stats_ref[0:8] = jnp.concatenate(picked, axis=0)
        stats_ref[8:16] = jnp.broadcast_to(total, (8, 128))
        gain_out_ref[...] = gain_ref[...].astype(jnp.float32).reshape(1, 8192)
        for copy in copies[3:]:
            copy.wait()

    anywhere = pl.BlockSpec(memory_space=pltpu.HBM)
    operands = (weight, hidden, floor_counts, gain, targets)
    return pl.pallas_call(
        body,
        out_shape=(
            pltpu.VMEM(weight.shape, jnp.bfloat16),
            pltpu.VMEM(hidden.shape, jnp.bfloat16),
            pltpu.VMEM((1024, 128), jnp.float32),
            pltpu.VMEM((1, 8192), jnp.float32),
            pltpu.VMEM((16, 128), jnp.float32),
        ),
        in_specs=[anywhere] * 5,
        out_specs=(VMEM,) * 5,
        scratch_shapes=[
            pltpu.VMEM((8, 1024), jnp.float32),
            pltpu.VMEM((1, entries), jnp.int32),
            pltpu.VMEM((8192,), jnp.bfloat16),
            pltpu.VMEM((8, 128), jnp.int32),
            pltpu.SemaphoreType.DMA((5,)),
        ],
        compiler_params=pltpu.CompilerParams(vmem_limit_bytes=2 << 20),
        name="prepare",
    )(*(pltpu.with_memory_space_constraint(operand, pltpu.HBM) for operand in operands))


def first_entry(entries):
    return (lax.axis_index(STREAM) * 8 + lax.axis_index(TENSOR)) * entries


def join_halves(products, floor_stats, targets):
    entries = products.shape[2]

    def body(products_ref, floors_ref, targets_ref, weights_ref, stats_ref):
        core = lax.rem(lax.axis_index(TENSOR), 2)
        first = first_entry(entries)
        rows = lax.broadcasted_iota(jnp.int32, (entries, 128), 0)
        left = lax.broadcasted_iota(jnp.int32, (entries, 128), 1) < 64
        weights_ref[1000:1024, :] = jnp.zeros((24, 1024), jnp.float32)
        for j in range(ROWS):
            x, z = j // 2, j % 2 * 2
            near = slice(x // 2 * 128, x // 2 * 128 + 128)
            one, two = products_ref[core, z, :, near], products_ref[core, z + 1, :, near]
            if x % 2 == 0:
                two = pltpu.roll(two, 64, 1)
            else:
                one = pltpu.roll(one, 64, 1)
            tile = products_ref[1 - core, x, :, z * 64:z * 64 + 128] + jnp.where(left, one, two)
            peak = jnp.max(tile, axis=0, keepdims=True)
            exponent = jnp.exp(tile - peak)
            weights_ref[0:entries, j * 128:(j + 1) * 128] = exponent
            hit = rows == targets_ref[j:j + 1, :] - first
            stats_ref[j:j + 1, :] = peak
            stats_ref[8 + j:9 + j, :] = jnp.sum(exponent, axis=0, keepdims=True)
            stats_ref[16 + j:17 + j, :] = jnp.sum(jnp.where(hit, exponent, 0.0), axis=0, keepdims=True)
        stats_ref[24:40, :] = floors_ref[...]

    return call(
        body,
        (
            jax.ShapeDtypeStruct((1024, 1024), jnp.float32),
            jax.ShapeDtypeStruct((40, 128), jnp.float32),
        ),
        "join_halves",
        (products, floor_stats, targets),
        vmem_mib=6,
        out_specs=(VMEM, VMEM),
    )


def join(axis, stats, before, last=None):
    size = SIZES[axis]
    hops = [0, 1] if size == 2 else [0, 1, 3, 2]
    pieces = [stats] + [shift(stats, axis, k, axis != "c") for k in hops[1:]]

    def body(*refs):
        piece_refs, rest = refs[:size], refs[size:]
        if before is not None:
            before_ref, rest = rest[0], rest[1:]
        held = rest[-1]
        mine = coordinate(axis)
        for piece_ref, k in zip(piece_refs, hops):
            held[lax.rem(mine - k + size, size)] = piece_ref[...]
        peak = held[0, 0:8]
        for i in range(1, size):
            peak = jnp.maximum(peak, held[i, 0:8])
        mass = target = floor = total = jnp.zeros((8, 128), jnp.float32)
        mass_before = total_before = jnp.zeros((8, 128), jnp.float32)
        if before is not None:
            mass_before = before_ref[0:8] * jnp.exp(piece_refs[0][0:8] - peak)
            total_before = before_ref[8:16]
        for i in range(size):
            scale = jnp.exp(held[i, 0:8] - peak)
            part = held[i, 8:16] * scale
            mass = mass + part
            target = target + held[i, 16:24] * scale
            floor = floor + held[i, 24:32]
            total = total + held[i, 32:40]
            earlier = i < mine
            mass_before = mass_before + jnp.where(earlier, part, 0.0)
            total_before = total_before + jnp.where(earlier, held[i, 32:40], 0.0)
        if last is None:
            stats_ref, after_ref = rest[0], rest[1]
            stats_ref[0:8] = peak
            stats_ref[8:16] = mass
            stats_ref[16:24] = target
            stats_ref[24:32] = floor
            stats_ref[32:40] = total
            after_ref[0:8] = mass_before
            after_ref[8:16] = total_before
        else:
            own_ref, totals_ref, terms_ref, bits_ref = rest[:4]
            tokens = totals_ref[...].astype(jnp.float32)
            free = (tokens - total) / mass
            terms_ref[0:8] = jnp.exp(own_ref[0:8] - peak) * free / tokens
            terms_ref[8:16] = 1.0 / tokens
            terms_ref[16:24] = (total_before + mass_before * free) / tokens
            bits_ref[...] = -jnp.log2((floor + target * free) / tokens)

    inputs = pieces + ([] if before is None else [before]) + ([] if last is None else list(last))
    first, second = ((40, 128), (16, 128)) if last is None else ((24, 128), (8, 128))
    return call(
        body,
        (jax.ShapeDtypeStruct(first, jnp.float32), jax.ShapeDtypeStruct(second, jnp.float32)),
        "join_" + axis,
        inputs,
        vmem_mib=2,
        scratch=[pltpu.VMEM((size, 40, 128), jnp.float32)],
        out_specs=(VMEM, VMEM),
    )


def running_sums(weights, floors):
    block = 256

    def body(weights_ref, floors_ref, sums_ref, floor_sums_ref):
        below = lax.broadcasted_iota(jnp.int32, (block, block), 1)
        lower = (below < lax.broadcasted_iota(jnp.int32, (block, block), 0)).astype(jnp.bfloat16)
        carry = [jnp.zeros((1, 256), jnp.float32)] * (ROWS // 2)
        floor_carry = jnp.zeros((1, 128), jnp.float32)
        for b in range(1024 // block):
            rows = slice(b * block, (b + 1) * block)
            floors = floors_ref[rows, :]
            floor_sums_ref[rows, :] = floor_carry + jnp.dot(
                lower, floors.astype(jnp.bfloat16), preferred_element_type=jnp.float32
            )
            floor_carry = floor_carry + jnp.sum(floors, axis=0, keepdims=True)
            for j in range(ROWS // 2):
                lanes = slice(j * 256, (j + 1) * 256)
                value = weights_ref[rows, lanes]
                high = value.astype(jnp.bfloat16)
                low = (value - high.astype(jnp.float32)).astype(jnp.bfloat16)
                sums = jnp.dot(lower, high, preferred_element_type=jnp.float32)
                sums = sums + jnp.dot(lower, low, preferred_element_type=jnp.float32)
                sums_ref[rows, lanes] = sums + carry[j]
                carry[j] = carry[j] + jnp.sum(value, axis=0, keepdims=True)

    return call(
        body,
        (
            jax.ShapeDtypeStruct((1024, 1024), jnp.float32),
            jax.ShapeDtypeStruct((1024, 128), jnp.float32),
        ),
        "running_sums",
        (weights, floors),
        vmem_mib=4,
        out_specs=(VMEM, VMEM),
    )


def finish(sums, floor_sums, terms, entries):
    def body(sums_ref, floors_ref, terms_ref, out_hbm, out_ref, sems):
        copies = []
        for j in range(ROWS):
            lanes = slice(j * 128, (j + 1) * 128)
            out_ref[:, lanes] = (
                sums_ref[0:entries, lanes] * terms_ref[j:j + 1, :]
                + floors_ref[0:entries, :] * terms_ref[8 + j:9 + j, :]
                + terms_ref[16 + j:17 + j, :]
            )
            copies.append(pltpu.make_async_copy(out_ref.at[:, lanes], out_hbm.at[:, lanes], sems.at[j]))
            copies[-1].start()
        for copy in copies:
            copy.wait()

    return call(
        body,
        jax.ShapeDtypeStruct((entries, 1024), jnp.float32),
        "finish",
        (sums, floor_sums, terms),
        vmem_mib=8,
        scratch=[pltpu.VMEM((entries, 1024), jnp.float32), pltpu.SemaphoreType.DMA((ROWS,))],
        out_specs=pl.BlockSpec(memory_space=pltpu.HBM),
    )


def own_coordinate(axes):
    core = lax.rem(lax.axis_index(TENSOR), 2)
    return jnp.where(core == 0, coordinate(axes[0]), coordinate(axes[1]))


def square_sums(pieces):
    def body(*refs):
        mine = coordinate("y")
        total = jnp.zeros((64, 1), jnp.float32)
        for i, k in enumerate((0, 1, 3, 2)):
            piece = refs[i][...]
            place = lax.rem(mine - k + 4, 4)
            refs[4][:, pl.ds(pl.multiple_of(place * 1024, 1024), 1024)] = piece
            widened = piece.astype(jnp.float32)
            total = total + jnp.sum(widened * widened, axis=1, keepdims=True)
        refs[5][...] = jnp.broadcast_to(total, (64, 128))

    return call(
        body,
        (jax.ShapeDtypeStruct((64, 4096), jnp.bfloat16), jax.ShapeDtypeStruct((64, 128), jnp.float32)),
        "square_sums",
        pieces,
        vmem_mib=4,
        out_specs=(VMEM, VMEM),
    )


def normalize(features, own, other, gain):
    def body(features_ref, own_ref, other_ref, gain_ref, upper_ref, lower_ref):
        core = lax.rem(lax.axis_index(TENSOR), 2)
        mean_square = (own_ref[:, 0:1] + other_ref[:, 0:1]) * (1.0 / 8192)
        scale = lax.rsqrt(mean_square + epsilon)
        for y in range(4):
            lanes = slice(y * 1024, (y + 1) * 1024)
            row = gain_ref[:, pl.ds(pl.multiple_of((y * 2 + core) * 1024, 1024), 1024)]
            value = (features_ref[:, lanes].astype(jnp.float32) * scale * row).astype(jnp.bfloat16)
            upper_ref[:, lanes] = value[:32]
            lower_ref[:, lanes] = value[32:]

    shape = jax.ShapeDtypeStruct((32, 4096), jnp.bfloat16)
    return call(
        body,
        (shape, shape),
        "normalize",
        (features, own, other, gain),
        vmem_mib=4,
        out_specs=(VMEM, VMEM),
    )


def stack(pieces, axes):
    rows = 2 * pieces[0][2].shape[0]
    half = rows // 2

    def body(*refs):
        mine = own_coordinate(axes)
        for (side, hops, _), ref in zip(pieces, refs):
            place = lax.rem(mine + (4 - hops), 4)
            refs[-3][pl.ds(pl.multiple_of(place * rows + side * half, half), half), :] = ref[...]
            for i, out_ref in enumerate(refs[-2:]):

                @pl.when(place // 2 == i)
                def _():
                    at = pl.multiple_of((place - 2 * i) * rows + side * half, half)
                    out_ref[pl.ds(at, half), :] = ref[...]

    whole = jax.ShapeDtypeStruct((4 * rows, 4096), jnp.bfloat16)
    shape = jax.ShapeDtypeStruct((2 * rows, 4096), jnp.bfloat16)
    return call(
        body,
        (whole, shape, shape),
        "stack",
        [piece[2] for piece in pieces],
        vmem_mib=4,
        out_specs=(VMEM, VMEM, VMEM),
    )


def multiply(weight, products, pieces, side, axes, keep=False):
    entries = weight.shape[0]
    arrays = [pieces[0][0]] if pieces[0][0] is pieces[1][0] else [piece[0] for piece in pieces]
    inputs = [weight] + ([] if products is None else [products]) + arrays

    def body(*refs):
        weight_ref, out_ref = refs[0], refs[len(inputs)]
        token_refs = refs[len(inputs) - len(arrays):len(inputs)]
        core = lax.rem(lax.axis_index(TENSOR), 2)
        features = core if side == 0 else 1 - core
        mine = coordinate_of(features, axes)
        total = None
        for y in range(4):
            far = pl.ds(pl.multiple_of((y * 2 + features) * 1024, 1024), 1024)
            value = [ref[:, y * 1024:(y + 1) * 1024] for ref in token_refs]
            value = value[0] if len(value) == 1 else jnp.concatenate(value, axis=0)
            if keep:
                refs[-1][:, y * 1024:(y + 1) * 1024] = value
            product = lax.dot_general(
                weight_ref[:, far], value, (((1,), (1,)), ((), ())), preferred_element_type=jnp.float32
            )
            total = product if total is None else total + product
        for i, (_, hops, half) in enumerate(pieces):
            place = lax.rem(mine + (4 - hops), 4)
            out_ref[side, place, :, half * 128:half * 128 + 128] = total[:, i * 128:i * 128 + 128]

    shape = jax.ShapeDtypeStruct((2, 4, entries, 256), jnp.float32)
    return call(
        body,
        (shape, jax.ShapeDtypeStruct((256, 4096), jnp.bfloat16)) if keep else shape,
        "multiply",
        inputs,
        vmem_mib=6,
        out_specs=(VMEM, VMEM) if keep else VMEM,
        input_output_aliases={} if products is None else {1: 0},
        cost_estimate=pl.CostEstimate(flops=2 * entries * 4096 * 256, bytes_accessed=4 << 20, transcendentals=0),
    )


def coordinate_of(core, axes):
    return jnp.where(core == 0, coordinate(axes[0]), coordinate(axes[1]))


def local(hidden, norm_gain, head_weight, floor_counts, totals, targets):
    weight = head_weight.T
    entries = weight.shape[0]
    targets = targets.reshape(8, 128)

    beside = [shift(hidden, "y", k) for k in (1, 3, 2)]
    weight, hidden, floors, gain, floor_stats = prepare(
        weight, hidden, floor_counts.reshape(1, entries), norm_gain, targets
    )
    weight, *beside = lax.optimization_barrier((weight, *beside))
    raw, own = square_sums([hidden] + beside)
    upper, lower = normalize(raw, own, shift(own, "c", 1), gain)
    axes = "xz"
    upper_1, lower_3 = shift(upper, axes, 1), shift(lower, axes, 3)
    upper_3, lower_1 = shift(upper, axes, 3), shift(lower, axes, 1)
    upper_2, lower_2 = shift(upper_1, axes, 1), shift(lower_3, axes, 3)
    pieces = [(0, 0, upper), (1, 0, lower), (0, 1, upper_1), (1, 3, lower_3)]
    pieces += [(0, 3, upper_3), (1, 1, lower_1), (0, 2, upper_2), (1, 2, lower_2)]
    block, upper, lower = stack(pieces, axes)

    axes = "zx"
    swap = lambda value: shift(value, "c", 1)
    up = lambda value: shift(value, axes, 1)
    down = lambda value: shift(value, axes, 3)
    hold = lax.optimization_barrier
    upper_1, lower_3 = up(upper), down(lower)
    swapped = swap(block)
    products = multiply(weight, None, [(block, 0, 0), (block, 0, 1)], 0, axes)
    upper, lower, products = hold((upper, lower, products))
    upper_3, lower_1 = down(upper), up(lower)
    products = multiply(weight, products, [(swapped, 0, 0), (swapped, 0, 1)], 1, axes)
    upper_1, lower_3, products = hold((upper_1, lower_3, products))
    upper_2, lower_2 = up(upper_1), down(lower_3)
    swapped_1 = swap(upper_1), swap(lower_3)
    products = multiply(weight, products, [(upper_1, 1, 0), (lower_3, 3, 1)], 0, axes)
    products = multiply(weight, products, [(upper_3, 3, 0), (lower_1, 1, 1)], 0, axes)
    upper_2, lower_2, upper_3, lower_1, products = hold((upper_2, lower_2, upper_3, lower_1, products))
    swapped_3 = swap(upper_3), swap(lower_1)
    swapped_2 = swap(upper_2), swap(lower_2)
    products = multiply(weight, products, [(upper_2, 2, 0), (lower_2, 2, 1)], 0, axes)
    products = multiply(weight, products, [(swapped_1[0], 1, 0), (swapped_1[1], 3, 1)], 1, axes)
    products = multiply(weight, products, [(swapped_3[0], 3, 0), (swapped_3[1], 1, 1)], 1, axes)
    products = multiply(weight, products, [(swapped_2[0], 2, 0), (swapped_2[1], 2, 1)], 1, axes)

    weights, stats = join_halves(products, floor_stats, targets)
    sums, floor_sums = running_sums(weights, floors)
    group, before = stats, None
    for axis in ("c", "y", "z"):
        group, before = join(axis, group, before)
    terms, bits = join("x", group, before, last=(stats, totals.reshape(8, 128)))
    cumulative = finish(sums, floor_sums, terms, entries)
    return cumulative.T, bits.reshape(1024)


def solution(mesh):
    in_specs = (P(STREAM, TENSOR), P(), P(None, BOTH), P(BOTH), P(), P())
    out_specs = (P(None, BOTH), P())
    return jax.shard_map(local, mesh=mesh, in_specs=in_specs, out_specs=out_specs, check_vma=False)
```

```python
import jax
import jax.numpy as jnp
from jax import lax
from jax.experimental import pallas as pl
from jax.experimental.pallas import tpu as pltpu
from jax.sharding import PartitionSpec as P

epsilon = 1e-05
STREAM, TENSOR = "stream", "tensor"
BOTH = (STREAM, TENSOR)
SIZES = {"x": 4, "z": 4, "y": 4, "c": 2}
STRIDES = {"x": 32, "z": 8, "y": 2, "c": 1}
ROWS = 8
VMEM = pl.BlockSpec(memory_space=pltpu.VMEM)


def coordinate(axis):
    index = lax.axis_index(STREAM) * 8 + lax.axis_index(TENSOR)
    return lax.rem(lax.div(index, STRIDES[axis]), SIZES[axis])


def shift(value, axis, hops, cross=False):
    pairs = []
    for source in range(128):
        name = axis[source % len(axis)]
        size, stride = SIZES[name], STRIDES[name]
        place = source // stride % size
        target = source + ((place + hops) % size - place) * stride
        pairs.append((source, target ^ 1 if cross else target))
    return lax.ppermute(value, BOTH, pairs)


def call(body, out_shape, name, inputs, vmem_mib=32, scratch=(), out_specs=VMEM, **rest):
    return pl.pallas_call(
        body,
        out_shape=out_shape,
        in_specs=[VMEM] * len(inputs),
        out_specs=out_specs,
        scratch_shapes=list(scratch),
        compiler_params=pltpu.CompilerParams(vmem_limit_bytes=vmem_mib << 20),
        name=name,
        **rest,
    )(*inputs)


def prepare(weight, hidden, floor_counts, gain, targets):
    entries = weight.shape[0]

    def body(weight_hbm, hidden_hbm, floors_hbm, gain_hbm, targets_hbm,
             weight_ref, hidden_ref, columns_ref, gain_out_ref, stats_ref,
             row, floors_ref, gain_ref, targets_ref, sems):
        copies = [
            pltpu.make_async_copy(source, target, sems.at[i])
            for i, (source, target) in enumerate((
                (floors_hbm, floors_ref),
                (targets_hbm, targets_ref),
                (gain_hbm, gain_ref),
                (hidden_hbm, hidden_ref),
                (weight_hbm, weight_ref),
            ))
        ]
        for copy in copies:
            copy.start()
        for copy in copies[:3]:
            copy.wait()
        row[...] = jnp.zeros_like(row)
        row[:, 0:entries] = jnp.broadcast_to(floors_ref[...].astype(jnp.float32), (8, entries))
        total = jnp.zeros((1, 128), jnp.float32)
        picked = [jnp.zeros((1, 128), jnp.float32)] * ROWS
        for b in range(ROWS):
            columns = jnp.transpose(jnp.concatenate([row[:, b * 128:(b + 1) * 128]] * 16, axis=0))
            columns_ref[b * 128:(b + 1) * 128, :] = columns
            total = total + jnp.sum(columns, axis=0, keepdims=True)
            rows = lax.broadcasted_iota(jnp.int32, (128, 128), 0) + (b * 128 + first_entry(entries))
            for j in range(ROWS):
                hit = jnp.where(rows == targets_ref[j:j + 1, :], columns, 0.0)
                picked[j] = picked[j] + jnp.sum(hit, axis=0, keepdims=True)
        stats_ref[0:8] = jnp.concatenate(picked, axis=0)
        stats_ref[8:16] = jnp.broadcast_to(total, (8, 128))
        gain_out_ref[...] = gain_ref[...].astype(jnp.float32).reshape(1, 8192)
        for copy in copies[3:]:
            copy.wait()

    anywhere = pl.BlockSpec(memory_space=pltpu.HBM)
    operands = (weight, hidden, floor_counts, gain, targets)
    return pl.pallas_call(
        body,
        out_shape=(
            pltpu.VMEM(weight.shape, jnp.bfloat16),
            pltpu.VMEM(hidden.shape, jnp.bfloat16),
            pltpu.VMEM((1024, 128), jnp.float32),
            pltpu.VMEM((1, 8192), jnp.float32),
            pltpu.VMEM((16, 128), jnp.float32),
        ),
        in_specs=[anywhere] * 5,
        out_specs=(VMEM,) * 5,
        scratch_shapes=[
            pltpu.VMEM((8, 1024), jnp.float32),
            pltpu.VMEM((1, entries), jnp.int32),
            pltpu.VMEM((8192,), jnp.bfloat16),
            pltpu.VMEM((8, 128), jnp.int32),
            pltpu.SemaphoreType.DMA((5,)),
        ],
        compiler_params=pltpu.CompilerParams(vmem_limit_bytes=2 << 20),
        name="prepare",
    )(*(pltpu.with_memory_space_constraint(operand, pltpu.HBM) for operand in operands))


def first_entry(entries):
    return (lax.axis_index(STREAM) * 8 + lax.axis_index(TENSOR)) * entries


def join_halves(products, floor_stats, targets):
    entries = products.shape[2]

    def body(products_ref, floors_ref, targets_ref, weights_ref, stats_ref):
        core = lax.rem(lax.axis_index(TENSOR), 2)
        first = first_entry(entries)
        rows = lax.broadcasted_iota(jnp.int32, (entries, 128), 0)
        left = lax.broadcasted_iota(jnp.int32, (entries, 128), 1) < 64
        weights_ref[1000:1024, :] = jnp.zeros((24, 1024), jnp.float32)
        for j in range(ROWS):
            x, z = j // 2, j % 2 * 2
            near = slice(x // 2 * 128, x // 2 * 128 + 128)
            one, two = products_ref[core, z, :, near], products_ref[core, z + 1, :, near]
            if x % 2 == 0:
                two = pltpu.roll(two, 64, 1)
            else:
                one = pltpu.roll(one, 64, 1)
            tile = products_ref[1 - core, x, :, z * 64:z * 64 + 128] + jnp.where(left, one, two)
            peak = jnp.max(tile, axis=0, keepdims=True)
            exponent = jnp.exp(tile - peak)
            weights_ref[0:entries, j * 128:(j + 1) * 128] = exponent
            hit = rows == targets_ref[j:j + 1, :] - first
            stats_ref[j:j + 1, :] = peak
            stats_ref[8 + j:9 + j, :] = jnp.sum(exponent, axis=0, keepdims=True)
            stats_ref[16 + j:17 + j, :] = jnp.sum(jnp.where(hit, exponent, 0.0), axis=0, keepdims=True)
        stats_ref[24:40, :] = floors_ref[...]

    return call(
        body,
        (
            jax.ShapeDtypeStruct((1024, 1024), jnp.float32),
            jax.ShapeDtypeStruct((40, 128), jnp.float32),
        ),
        "join_halves",
        (products, floor_stats, targets),
        vmem_mib=6,
        out_specs=(VMEM, VMEM),
    )


def join(axis, stats, before, last=None):
    size = SIZES[axis]
    hops = [0, 1] if size == 2 else [0, 1, 3, 2]
    pieces = [stats] + [shift(stats, axis, k, axis != "c") for k in hops[1:]]

    def body(*refs):
        piece_refs, rest = refs[:size], refs[size:]
        if before is not None:
            before_ref, rest = rest[0], rest[1:]
        held = rest[-1]
        mine = coordinate(axis)
        for piece_ref, k in zip(piece_refs, hops):
            held[lax.rem(mine - k + size, size)] = piece_ref[...]
        peak = held[0, 0:8]
        for i in range(1, size):
            peak = jnp.maximum(peak, held[i, 0:8])
        mass = target = floor = total = jnp.zeros((8, 128), jnp.float32)
        mass_before = total_before = jnp.zeros((8, 128), jnp.float32)
        if before is not None:
            mass_before = before_ref[0:8] * jnp.exp(piece_refs[0][0:8] - peak)
            total_before = before_ref[8:16]
        for i in range(size):
            scale = jnp.exp(held[i, 0:8] - peak)
            part = held[i, 8:16] * scale
            mass = mass + part
            target = target + held[i, 16:24] * scale
            floor = floor + held[i, 24:32]
            total = total + held[i, 32:40]
            earlier = i < mine
            mass_before = mass_before + jnp.where(earlier, part, 0.0)
            total_before = total_before + jnp.where(earlier, held[i, 32:40], 0.0)
        if last is None:
            stats_ref, after_ref = rest[0], rest[1]
            stats_ref[0:8] = peak
            stats_ref[8:16] = mass
            stats_ref[16:24] = target
            stats_ref[24:32] = floor
            stats_ref[32:40] = total
            after_ref[0:8] = mass_before
            after_ref[8:16] = total_before
        else:
            own_ref, totals_ref, terms_ref, bits_ref = rest[:4]
            tokens = totals_ref[...].astype(jnp.float32)
            free = (tokens - total) / mass
            terms_ref[0:8] = jnp.exp(own_ref[0:8] - peak) * free / tokens
            terms_ref[8:16] = 1.0 / tokens
            terms_ref[16:24] = (total_before + mass_before * free) / tokens
            bits_ref[...] = -jnp.log2((floor + target * free) / tokens)

    inputs = pieces + ([] if before is None else [before]) + ([] if last is None else list(last))
    first, second = ((40, 128), (16, 128)) if last is None else ((24, 128), (8, 128))
    return call(
        body,
        (jax.ShapeDtypeStruct(first, jnp.float32), jax.ShapeDtypeStruct(second, jnp.float32)),
        "join_" + axis,
        inputs,
        vmem_mib=2,
        scratch=[pltpu.VMEM((size, 40, 128), jnp.float32)],
        out_specs=(VMEM, VMEM),
    )


def running_sums(weights, floors):
    block = 256

    def body(weights_ref, floors_ref, sums_ref, floor_sums_ref):
        below = lax.broadcasted_iota(jnp.int32, (block, block), 1)
        lower = (below < lax.broadcasted_iota(jnp.int32, (block, block), 0)).astype(jnp.bfloat16)
        carry = [jnp.zeros((1, 256), jnp.float32)] * (ROWS // 2)
        floor_carry = jnp.zeros((1, 128), jnp.float32)
        for b in range(1024 // block):
            rows = slice(b * block, (b + 1) * block)
            floors = floors_ref[rows, :]
            floor_sums_ref[rows, :] = floor_carry + jnp.dot(
                lower, floors.astype(jnp.bfloat16), preferred_element_type=jnp.float32
            )
            floor_carry = floor_carry + jnp.sum(floors, axis=0, keepdims=True)
            for j in range(ROWS // 2):
                lanes = slice(j * 256, (j + 1) * 256)
                value = weights_ref[rows, lanes]
                high = value.astype(jnp.bfloat16)
                low = (value - high.astype(jnp.float32)).astype(jnp.bfloat16)
                sums = jnp.dot(lower, high, preferred_element_type=jnp.float32)
                sums = sums + jnp.dot(lower, low, preferred_element_type=jnp.float32)
                sums_ref[rows, lanes] = sums + carry[j]
                carry[j] = carry[j] + jnp.sum(value, axis=0, keepdims=True)

    return call(
        body,
        (
            jax.ShapeDtypeStruct((1024, 1024), jnp.float32),
            jax.ShapeDtypeStruct((1024, 128), jnp.float32),
        ),
        "running_sums",
        (weights, floors),
        vmem_mib=4,
        out_specs=(VMEM, VMEM),
    )


def finish(sums, floor_sums, terms, entries):
    def body(sums_ref, floors_ref, terms_ref, out_hbm, out_ref, sems):
        copies = []
        for j in range(ROWS):
            lanes = slice(j * 128, (j + 1) * 128)
            out_ref[:, lanes] = (
                sums_ref[0:entries, lanes] * terms_ref[j:j + 1, :]
                + floors_ref[0:entries, :] * terms_ref[8 + j:9 + j, :]
                + terms_ref[16 + j:17 + j, :]
            )
            copies.append(pltpu.make_async_copy(out_ref.at[:, lanes], out_hbm.at[:, lanes], sems.at[j]))
            copies[-1].start()
        for copy in copies:
            copy.wait()

    return call(
        body,
        jax.ShapeDtypeStruct((entries, 1024), jnp.float32),
        "finish",
        (sums, floor_sums, terms),
        vmem_mib=8,
        scratch=[pltpu.VMEM((entries, 1024), jnp.float32), pltpu.SemaphoreType.DMA((ROWS,))],
        out_specs=pl.BlockSpec(memory_space=pltpu.HBM),
    )


def own_coordinate(axes):
    core = lax.rem(lax.axis_index(TENSOR), 2)
    return jnp.where(core == 0, coordinate(axes[0]), coordinate(axes[1]))


def square_sums(pieces):
    def body(*refs):
        mine = coordinate("y")
        total = jnp.zeros((64, 1), jnp.float32)
        for i, k in enumerate((0, 1, 3, 2)):
            piece = refs[i][...]
            place = lax.rem(mine - k + 4, 4)
            refs[4][:, pl.ds(pl.multiple_of(place * 1024, 1024), 1024)] = piece
            widened = piece.astype(jnp.float32)
            total = total + jnp.sum(widened * widened, axis=1, keepdims=True)
        refs[5][...] = jnp.broadcast_to(total, (64, 128))

    return call(
        body,
        (jax.ShapeDtypeStruct((64, 4096), jnp.bfloat16), jax.ShapeDtypeStruct((64, 128), jnp.float32)),
        "square_sums",
        pieces,
        vmem_mib=4,
        out_specs=(VMEM, VMEM),
    )


def normalize(features, own, other, gain):
    def body(features_ref, own_ref, other_ref, gain_ref, upper_ref, lower_ref):
        core = lax.rem(lax.axis_index(TENSOR), 2)
        mean_square = (own_ref[:, 0:1] + other_ref[:, 0:1]) * (1.0 / 8192)
        scale = lax.rsqrt(mean_square + epsilon)
        for y in range(4):
            lanes = slice(y * 1024, (y + 1) * 1024)
            row = gain_ref[:, pl.ds(pl.multiple_of((y * 2 + core) * 1024, 1024), 1024)]
            value = (features_ref[:, lanes].astype(jnp.float32) * scale * row).astype(jnp.bfloat16)
            upper_ref[:, lanes] = value[:32]
            lower_ref[:, lanes] = value[32:]

    shape = jax.ShapeDtypeStruct((32, 4096), jnp.bfloat16)
    return call(
        body,
        (shape, shape),
        "normalize",
        (features, own, other, gain),
        vmem_mib=4,
        out_specs=(VMEM, VMEM),
    )


def stack(pieces, axes):
    rows = 2 * pieces[0][2].shape[0]
    half = rows // 2

    def body(*refs):
        mine = own_coordinate(axes)
        for (side, hops, _), ref in zip(pieces, refs):
            place = lax.rem(mine + (4 - hops), 4)
            refs[-3][pl.ds(pl.multiple_of(place * rows + side * half, half), half), :] = ref[...]
            for i, out_ref in enumerate(refs[-2:]):

                @pl.when(place // 2 == i)
                def _():
                    at = pl.multiple_of((place - 2 * i) * rows + side * half, half)
                    out_ref[pl.ds(at, half), :] = ref[...]

    whole = jax.ShapeDtypeStruct((4 * rows, 4096), jnp.bfloat16)
    shape = jax.ShapeDtypeStruct((2 * rows, 4096), jnp.bfloat16)
    return call(
        body,
        (whole, shape, shape),
        "stack",
        [piece[2] for piece in pieces],
        vmem_mib=4,
        out_specs=(VMEM, VMEM, VMEM),
    )


def multiply(weight, products, pieces, side, axes, keep=False, cost=1):
    entries = weight.shape[0]
    arrays = [pieces[0][0]] if pieces[0][0] is pieces[1][0] else [piece[0] for piece in pieces]
    inputs = [weight] + ([] if products is None else [products]) + arrays

    def body(*refs):
        weight_ref, out_ref = refs[0], refs[len(inputs)]
        token_refs = refs[len(inputs) - len(arrays):len(inputs)]
        core = lax.rem(lax.axis_index(TENSOR), 2)
        features = core if side == 0 else 1 - core
        mine = coordinate_of(features, axes)
        total = None
        for y in range(4):
            far = pl.ds(pl.multiple_of((y * 2 + features) * 1024, 1024), 1024)
            value = [ref[:, y * 1024:(y + 1) * 1024] for ref in token_refs]
            value = value[0] if len(value) == 1 else jnp.concatenate(value, axis=0)
            if keep:
                refs[-1][:, y * 1024:(y + 1) * 1024] = value
            product = lax.dot_general(
                weight_ref[:, far], value, (((1,), (1,)), ((), ())), preferred_element_type=jnp.float32
            )
            total = product if total is None else total + product
        for i, (_, hops, half) in enumerate(pieces):
            place = lax.rem(mine + (4 - hops), 4)
            out_ref[side, place, :, half * 128:half * 128 + 128] = total[:, i * 128:i * 128 + 128]

    shape = jax.ShapeDtypeStruct((2, 4, entries, 256), jnp.float32)
    return call(
        body,
        (shape, jax.ShapeDtypeStruct((256, 4096), jnp.bfloat16)) if keep else shape,
        "multiply",
        inputs,
        vmem_mib=6,
        out_specs=(VMEM, VMEM) if keep else VMEM,
        input_output_aliases={} if products is None else {1: 0},
        cost_estimate=pl.CostEstimate(
            flops=cost * 2 * entries * 4096 * 256, bytes_accessed=4 << 20, transcendentals=0
        ),
    )


def beside_each(upper, lower):
    def body(upper_ref, lower_ref, out_ref):
        out_ref[0:128, :] = upper_ref[...]
        out_ref[128:256, :] = lower_ref[...]

    shape = jax.ShapeDtypeStruct((256, 4096), jnp.bfloat16)
    return call(body, shape, "beside_each", (upper, lower), vmem_mib=2)


def coordinate_of(core, axes):
    return jnp.where(core == 0, coordinate(axes[0]), coordinate(axes[1]))


def local(hidden, norm_gain, head_weight, floor_counts, totals, targets):
    weight = head_weight.T
    entries = weight.shape[0]
    targets = targets.reshape(8, 128)

    beside = [shift(hidden, "y", k) for k in (1, 3, 2)]
    weight, hidden, floors, gain, floor_stats = prepare(
        weight, hidden, floor_counts.reshape(1, entries), norm_gain, targets
    )
    weight, *beside = lax.optimization_barrier((weight, *beside))
    raw, own = square_sums([hidden] + beside)
    upper, lower = normalize(raw, own, shift(own, "c", 1), gain)
    axes = "xz"
    upper_1, lower_3 = shift(upper, axes, 1), shift(lower, axes, 3)
    upper_3, lower_1 = shift(upper, axes, 3), shift(lower, axes, 1)
    upper_2, lower_2 = shift(upper_1, axes, 1), shift(lower_3, axes, 3)
    pieces = [(0, 0, upper), (1, 0, lower), (0, 1, upper_1), (1, 3, lower_3)]
    pieces += [(0, 3, upper_3), (1, 1, lower_1), (0, 2, upper_2), (1, 2, lower_2)]
    block, upper, lower = stack(pieces, axes)

    axes = "zx"
    swap = lambda value: shift(value, "c", 1)
    up = lambda value: shift(value, axes, 1)
    down = lambda value: shift(value, axes, 3)
    hold = lax.optimization_barrier
    upper_1, lower_3 = up(upper), down(lower)
    swapped = swap(block)
    products = multiply(weight, None, [(block, 0, 0), (block, 0, 1)], 0, axes)
    upper, lower, products = hold((upper, lower, products))
    upper_3, lower_1 = down(upper), up(lower)
    products = multiply(weight, products, [(swapped, 0, 0), (swapped, 0, 1)], 1, axes)
    upper_1, lower_3, products = hold((upper_1, lower_3, products))
    upper_2, lower_2 = up(upper_1), down(lower_3)
    pair_1 = swap(beside_each(upper_1, lower_3))
    products = multiply(weight, products, [(upper_1, 1, 0), (lower_3, 3, 1)], 0, axes)
    products = multiply(weight, products, [(upper_3, 3, 0), (lower_1, 1, 1)], 0, axes, cost=10)
    products = multiply(weight, products, [(pair_1, 1, 0), (pair_1, 3, 1)], 1, axes)
    upper_2, lower_2, upper_3, lower_1, products = hold((upper_2, lower_2, upper_3, lower_1, products))
    swapped_3 = swap(upper_3), swap(lower_1)
    swapped_2 = swap(upper_2), swap(lower_2)
    products = multiply(weight, products, [(upper_2, 2, 0), (lower_2, 2, 1)], 0, axes)
    products = multiply(weight, products, [(swapped_3[0], 3, 0), (swapped_3[1], 1, 1)], 1, axes)
    products = multiply(weight, products, [(swapped_2[0], 2, 0), (swapped_2[1], 2, 1)], 1, axes)

    weights, stats = join_halves(products, floor_stats, targets)
    sums, floor_sums = running_sums(weights, floors)
    group, before = stats, None
    for axis in ("c", "y", "z"):
        group, before = join(axis, group, before)
    terms, bits = join("x", group, before, last=(stats, totals.reshape(8, 128)))
    cumulative = finish(sums, floor_sums, terms, entries)
    return cumulative.T, bits.reshape(1024)


def solution(mesh):
    in_specs = (P(STREAM, TENSOR), P(), P(None, BOTH), P(BOTH), P(), P())
    out_specs = (P(None, BOTH), P())
    return jax.shard_map(local, mesh=mesh, in_specs=in_specs, out_specs=out_specs, check_vma=False)
```

```python
import jax
import jax.numpy as jnp
from jax import lax
from jax.experimental import pallas as pl
from jax.experimental.pallas import tpu as pltpu
from jax.sharding import PartitionSpec as P

epsilon = 1e-05
STREAM, TENSOR = "stream", "tensor"
BOTH = (STREAM, TENSOR)
SIZES = {"x": 4, "z": 4, "y": 4, "c": 2}
STRIDES = {"x": 32, "z": 8, "y": 2, "c": 1}
ROWS = 8
VMEM = pl.BlockSpec(memory_space=pltpu.VMEM)


def coordinate(axis):
    index = lax.axis_index(STREAM) * 8 + lax.axis_index(TENSOR)
    return lax.rem(lax.div(index, STRIDES[axis]), SIZES[axis])


def shift(value, axis, hops, cross=False):
    pairs = []
    for source in range(128):
        name = axis[source % len(axis)]
        size, stride = SIZES[name], STRIDES[name]
        place = source // stride % size
        target = source + ((place + hops) % size - place) * stride
        pairs.append((source, target ^ 1 if cross else target))
    return lax.ppermute(value, BOTH, pairs)


def call(body, out_shape, name, inputs, vmem_mib=32, scratch=(), out_specs=VMEM, **rest):
    return pl.pallas_call(
        body,
        out_shape=out_shape,
        in_specs=[VMEM] * len(inputs),
        out_specs=out_specs,
        scratch_shapes=list(scratch),
        compiler_params=pltpu.CompilerParams(vmem_limit_bytes=vmem_mib << 20),
        name=name,
        **rest,
    )(*inputs)


def prepare(weight, hidden, floor_counts, gain, targets):
    entries = weight.shape[0]

    def body(weight_hbm, hidden_hbm, floors_hbm, gain_hbm, targets_hbm,
             weight_ref, hidden_ref, columns_ref, gain_out_ref, stats_ref,
             row, floors_ref, gain_ref, targets_ref, sems):
        copies = [
            pltpu.make_async_copy(source, target, sems.at[i])
            for i, (source, target) in enumerate((
                (floors_hbm, floors_ref),
                (targets_hbm, targets_ref),
                (gain_hbm, gain_ref),
                (hidden_hbm, hidden_ref),
                (weight_hbm, weight_ref),
            ))
        ]
        for copy in copies:
            copy.start()
        for copy in copies[:3]:
            copy.wait()
        row[...] = jnp.zeros_like(row)
        row[:, 0:entries] = jnp.broadcast_to(floors_ref[...].astype(jnp.float32), (8, entries))
        total = jnp.zeros((1, 128), jnp.float32)
        picked = [jnp.zeros((1, 128), jnp.float32)] * ROWS
        for b in range(ROWS):
            columns = jnp.transpose(jnp.concatenate([row[:, b * 128:(b + 1) * 128]] * 16, axis=0))
            columns_ref[b * 128:(b + 1) * 128, :] = columns
            total = total + jnp.sum(columns, axis=0, keepdims=True)
            rows = lax.broadcasted_iota(jnp.int32, (128, 128), 0) + (b * 128 + first_entry(entries))
            for j in range(ROWS):
                hit = jnp.where(rows == targets_ref[j:j + 1, :], columns, 0.0)
                picked[j] = picked[j] + jnp.sum(hit, axis=0, keepdims=True)
        stats_ref[0:8] = jnp.concatenate(picked, axis=0)
        stats_ref[8:16] = jnp.broadcast_to(total, (8, 128))
        gain_out_ref[...] = gain_ref[...].astype(jnp.float32).reshape(1, 8192)
        for copy in copies[3:]:
            copy.wait()

    anywhere = pl.BlockSpec(memory_space=pltpu.HBM)
    operands = (weight, hidden, floor_counts, gain, targets)
    return pl.pallas_call(
        body,
        out_shape=(
            pltpu.VMEM(weight.shape, jnp.bfloat16),
            pltpu.VMEM(hidden.shape, jnp.bfloat16),
            pltpu.VMEM((1024, 128), jnp.float32),
            pltpu.VMEM((1, 8192), jnp.float32),
            pltpu.VMEM((16, 128), jnp.float32),
        ),
        in_specs=[anywhere] * 5,
        out_specs=(VMEM,) * 5,
        scratch_shapes=[
            pltpu.VMEM((8, 1024), jnp.float32),
            pltpu.VMEM((1, entries), jnp.int32),
            pltpu.VMEM((8192,), jnp.bfloat16),
            pltpu.VMEM((8, 128), jnp.int32),
            pltpu.SemaphoreType.DMA((5,)),
        ],
        compiler_params=pltpu.CompilerParams(vmem_limit_bytes=2 << 20),
        name="prepare",
    )(*(pltpu.with_memory_space_constraint(operand, pltpu.HBM) for operand in operands))


def first_entry(entries):
    return (lax.axis_index(STREAM) * 8 + lax.axis_index(TENSOR)) * entries


def join_halves(products, floor_stats, targets):
    entries = products.shape[2]

    def body(products_ref, floors_ref, targets_ref, weights_ref, stats_ref):
        core = lax.rem(lax.axis_index(TENSOR), 2)
        first = first_entry(entries)
        rows = lax.broadcasted_iota(jnp.int32, (entries, 128), 0)
        left = lax.broadcasted_iota(jnp.int32, (entries, 128), 1) < 64
        weights_ref[1000:1024, :] = jnp.zeros((24, 1024), jnp.float32)
        for j in range(ROWS):
            x, z = j // 2, j % 2 * 2
            near = slice(x // 2 * 128, x // 2 * 128 + 128)
            one, two = products_ref[core, z, :, near], products_ref[core, z + 1, :, near]
            if x % 2 == 0:
                two = pltpu.roll(two, 64, 1)
            else:
                one = pltpu.roll(one, 64, 1)
            tile = products_ref[1 - core, x, :, z * 64:z * 64 + 128] + jnp.where(left, one, two)
            peak = jnp.max(tile, axis=0, keepdims=True)
            exponent = jnp.exp(tile - peak)
            weights_ref[0:entries, j * 128:(j + 1) * 128] = exponent
            hit = rows == targets_ref[j:j + 1, :] - first
            stats_ref[j:j + 1, :] = peak
            stats_ref[8 + j:9 + j, :] = jnp.sum(exponent, axis=0, keepdims=True)
            stats_ref[16 + j:17 + j, :] = jnp.sum(jnp.where(hit, exponent, 0.0), axis=0, keepdims=True)
        stats_ref[24:40, :] = floors_ref[...]

    return call(
        body,
        (
            jax.ShapeDtypeStruct((1024, 1024), jnp.float32),
            jax.ShapeDtypeStruct((40, 128), jnp.float32),
        ),
        "join_halves",
        (products, floor_stats, targets),
        vmem_mib=6,
        out_specs=(VMEM, VMEM),
    )


def join(axis, stats, before, last=None):
    size = SIZES[axis]
    hops = [0, 1] if size == 2 else [0, 1, 3, 2]
    pieces = [stats] + [shift(stats, axis, k, axis != "c") for k in hops[1:]]

    def body(*refs):
        piece_refs, rest = refs[:size], refs[size:]
        if before is not None:
            before_ref, rest = rest[0], rest[1:]
        held = rest[-1]
        mine = coordinate(axis)
        for piece_ref, k in zip(piece_refs, hops):
            held[lax.rem(mine - k + size, size)] = piece_ref[...]
        peak = held[0, 0:8]
        for i in range(1, size):
            peak = jnp.maximum(peak, held[i, 0:8])
        mass = target = floor = total = jnp.zeros((8, 128), jnp.float32)
        mass_before = total_before = jnp.zeros((8, 128), jnp.float32)
        if before is not None:
            mass_before = before_ref[0:8] * jnp.exp(piece_refs[0][0:8] - peak)
            total_before = before_ref[8:16]
        for i in range(size):
            scale = jnp.exp(held[i, 0:8] - peak)
            part = held[i, 8:16] * scale
            mass = mass + part
            target = target + held[i, 16:24] * scale
            floor = floor + held[i, 24:32]
            total = total + held[i, 32:40]
            earlier = i < mine
            mass_before = mass_before + jnp.where(earlier, part, 0.0)
            total_before = total_before + jnp.where(earlier, held[i, 32:40], 0.0)
        if last is None:
            stats_ref, after_ref = rest[0], rest[1]
            stats_ref[0:8] = peak
            stats_ref[8:16] = mass
            stats_ref[16:24] = target
            stats_ref[24:32] = floor
            stats_ref[32:40] = total
            after_ref[0:8] = mass_before
            after_ref[8:16] = total_before
        else:
            own_ref, totals_ref, terms_ref = rest[:3]
            tokens = totals_ref[...].astype(jnp.float32)
            free = (tokens - total) / mass
            terms_ref[0:8] = jnp.exp(own_ref[0:8] - peak) * free / tokens
            terms_ref[8:16] = 1.0 / tokens
            terms_ref[16:24] = (total_before + mass_before * free) / tokens
            terms_ref[24:32] = -jnp.log2((floor + target * free) / tokens)

    inputs = pieces + ([] if before is None else [before]) + ([] if last is None else list(last))
    shapes = ((40, 128), (16, 128)) if last is None else ((32, 128),)
    return call(
        body,
        tuple(jax.ShapeDtypeStruct(shape, jnp.float32) for shape in shapes),
        "join_" + axis,
        inputs,
        vmem_mib=2,
        scratch=[pltpu.VMEM((size, 40, 128), jnp.float32)],
        out_specs=(VMEM,) * len(shapes),
    )


def running_sums(weights, floors):
    block = 256

    def body(weights_ref, floors_ref, sums_ref, floor_sums_ref):
        below = lax.broadcasted_iota(jnp.int32, (block, block), 1)
        lower = (below < lax.broadcasted_iota(jnp.int32, (block, block), 0)).astype(jnp.bfloat16)
        carry = [jnp.zeros((1, 256), jnp.float32)] * (ROWS // 2)
        floor_carry = jnp.zeros((1, 128), jnp.float32)
        for b in range(1024 // block):
            rows = slice(b * block, (b + 1) * block)
            floors = floors_ref[rows, :]
            floor_sums_ref[rows, :] = floor_carry + jnp.dot(
                lower, floors.astype(jnp.bfloat16), preferred_element_type=jnp.float32
            )
            floor_carry = floor_carry + jnp.sum(floors, axis=0, keepdims=True)
            for j in range(ROWS // 2):
                lanes = slice(j * 256, (j + 1) * 256)
                value = weights_ref[rows, lanes]
                high = value.astype(jnp.bfloat16)
                low = (value - high.astype(jnp.float32)).astype(jnp.bfloat16)
                sums = jnp.dot(lower, high, preferred_element_type=jnp.float32)
                sums = sums + jnp.dot(lower, low, preferred_element_type=jnp.float32)
                sums_ref[rows, lanes] = sums + carry[j]
                carry[j] = carry[j] + jnp.sum(value, axis=0, keepdims=True)

    return call(
        body,
        (
            jax.ShapeDtypeStruct((1024, 1024), jnp.float32),
            jax.ShapeDtypeStruct((1024, 128), jnp.float32),
        ),
        "running_sums",
        (weights, floors),
        vmem_mib=4,
        out_specs=(VMEM, VMEM),
    )


def finish(sums, floor_sums, terms, entries):
    def body(sums_ref, floors_ref, terms_ref, out_hbm, bits_hbm, out_ref, sems):
        copies = [pltpu.make_async_copy(terms_ref.at[24:32], bits_hbm, sems.at[ROWS])]
        copies[0].start()
        for j in range(ROWS):
            lanes = slice(j * 128, (j + 1) * 128)
            out_ref[:, lanes] = (
                sums_ref[0:entries, lanes] * terms_ref[j:j + 1, :]
                + floors_ref[0:entries, :] * terms_ref[8 + j:9 + j, :]
                + terms_ref[16 + j:17 + j, :]
            )
            copies.append(pltpu.make_async_copy(out_ref.at[:, lanes], out_hbm.at[:, lanes], sems.at[j]))
            copies[-1].start()
        for copy in copies:
            copy.wait()

    return call(
        body,
        (
            jax.ShapeDtypeStruct((entries, 1024), jnp.float32),
            jax.ShapeDtypeStruct((8, 128), jnp.float32),
        ),
        "finish",
        (sums, floor_sums, terms),
        vmem_mib=8,
        scratch=[pltpu.VMEM((entries, 1024), jnp.float32), pltpu.SemaphoreType.DMA((ROWS + 1,))],
        out_specs=(pl.BlockSpec(memory_space=pltpu.HBM),) * 2,
    )


def own_coordinate(axes):
    core = lax.rem(lax.axis_index(TENSOR), 2)
    return jnp.where(core == 0, coordinate(axes[0]), coordinate(axes[1]))


def square_sums(pieces):
    def body(*refs):
        mine = coordinate("y")
        total = jnp.zeros((64, 1), jnp.float32)
        for i, k in enumerate((0, 1, 3, 2)):
            piece = refs[i][...]
            place = lax.rem(mine - k + 4, 4)
            refs[4][:, pl.ds(pl.multiple_of(place * 1024, 1024), 1024)] = piece
            widened = piece.astype(jnp.float32)
            total = total + jnp.sum(widened * widened, axis=1, keepdims=True)
        refs[5][...] = jnp.broadcast_to(total, (64, 128))

    return call(
        body,
        (jax.ShapeDtypeStruct((64, 4096), jnp.bfloat16), jax.ShapeDtypeStruct((64, 128), jnp.float32)),
        "square_sums",
        pieces,
        vmem_mib=4,
        out_specs=(VMEM, VMEM),
    )


def normalize(features, own, other, gain):
    def body(features_ref, own_ref, other_ref, gain_ref, upper_ref, lower_ref):
        core = lax.rem(lax.axis_index(TENSOR), 2)
        mean_square = (own_ref[:, 0:1] + other_ref[:, 0:1]) * (1.0 / 8192)
        scale = lax.rsqrt(mean_square + epsilon)
        for y in range(4):
            lanes = slice(y * 1024, (y + 1) * 1024)
            row = gain_ref[:, pl.ds(pl.multiple_of((y * 2 + core) * 1024, 1024), 1024)]
            value = (features_ref[:, lanes].astype(jnp.float32) * scale * row).astype(jnp.bfloat16)
            upper_ref[:, lanes] = value[:32]
            lower_ref[:, lanes] = value[32:]

    shape = jax.ShapeDtypeStruct((32, 4096), jnp.bfloat16)
    return call(
        body,
        (shape, shape),
        "normalize",
        (features, own, other, gain),
        vmem_mib=4,
        out_specs=(VMEM, VMEM),
    )


def stack(pieces, axes):
    rows = 2 * pieces[0][2].shape[0]
    half = rows // 2

    def body(*refs):
        mine = own_coordinate(axes)
        for (side, hops, _), ref in zip(pieces, refs):
            place = lax.rem(mine + (4 - hops), 4)
            refs[-3][pl.ds(pl.multiple_of(place * rows + side * half, half), half), :] = ref[...]
            for i, out_ref in enumerate(refs[-2:]):

                @pl.when(place // 2 == i)
                def _():
                    at = pl.multiple_of((place - 2 * i) * rows + side * half, half)
                    out_ref[pl.ds(at, half), :] = ref[...]

    whole = jax.ShapeDtypeStruct((4 * rows, 4096), jnp.bfloat16)
    shape = jax.ShapeDtypeStruct((2 * rows, 4096), jnp.bfloat16)
    return call(
        body,
        (whole, shape, shape),
        "stack",
        [piece[2] for piece in pieces],
        vmem_mib=4,
        out_specs=(VMEM, VMEM, VMEM),
    )


def multiply(weight, products, pieces, side, axes, cost=1):
    entries = weight.shape[0]
    arrays = [pieces[0][0]] if pieces[0][0] is pieces[1][0] else [piece[0] for piece in pieces]
    inputs = [weight] + ([] if products is None else [products]) + arrays

    def body(*refs):
        weight_ref, out_ref = refs[0], refs[len(inputs)]
        token_refs = refs[len(inputs) - len(arrays):len(inputs)]
        core = lax.rem(lax.axis_index(TENSOR), 2)
        features = core if side == 0 else 1 - core
        mine = coordinate_of(features, axes)
        total = None
        for y in range(4):
            far = pl.ds(pl.multiple_of((y * 2 + features) * 1024, 1024), 1024)
            value = [ref[:, y * 1024:(y + 1) * 1024] for ref in token_refs]
            value = value[0] if len(value) == 1 else jnp.concatenate(value, axis=0)
            product = lax.dot_general(
                weight_ref[:, far], value, (((1,), (1,)), ((), ())), preferred_element_type=jnp.float32
            )
            total = product if total is None else total + product
        for i, (_, hops, half) in enumerate(pieces):
            place = lax.rem(mine + (4 - hops), 4)
            out_ref[side, place, :, half * 128:half * 128 + 128] = total[:, i * 128:i * 128 + 128]

    shape = jax.ShapeDtypeStruct((2, 4, entries, 256), jnp.float32)
    return call(
        body,
        shape,
        "multiply",
        inputs,
        vmem_mib=6,
        input_output_aliases={} if products is None else {1: 0},
        cost_estimate=pl.CostEstimate(
            flops=cost * 2 * entries * 4096 * 256, bytes_accessed=4 << 20, transcendentals=0
        ),
    )


def beside_each(upper, lower):
    def body(upper_ref, lower_ref, out_ref):
        out_ref[0:128, :] = upper_ref[...]
        out_ref[128:256, :] = lower_ref[...]

    shape = jax.ShapeDtypeStruct((256, 4096), jnp.bfloat16)
    return call(body, shape, "beside_each", (upper, lower), vmem_mib=2)


def coordinate_of(core, axes):
    return jnp.where(core == 0, coordinate(axes[0]), coordinate(axes[1]))


def local(hidden, norm_gain, head_weight, floor_counts, totals, targets):
    weight = head_weight.T
    entries = weight.shape[0]
    targets = targets.reshape(8, 128)

    beside = [shift(hidden, "y", k) for k in (1, 3, 2)]
    weight, hidden, floors, gain, floor_stats = prepare(
        weight, hidden, floor_counts.reshape(1, entries), norm_gain, targets
    )
    weight, *beside = lax.optimization_barrier((weight, *beside))
    raw, own = square_sums([hidden] + beside)
    upper, lower = normalize(raw, own, shift(own, "c", 1), gain)
    axes = "xz"
    upper_1, lower_3 = shift(upper, axes, 1), shift(lower, axes, 3)
    upper_3, lower_1 = shift(upper, axes, 3), shift(lower, axes, 1)
    upper_2, lower_2 = shift(upper_1, axes, 1), shift(lower_3, axes, 3)
    pieces = [(0, 0, upper), (1, 0, lower), (0, 1, upper_1), (1, 3, lower_3)]
    pieces += [(0, 3, upper_3), (1, 1, lower_1), (0, 2, upper_2), (1, 2, lower_2)]
    block, upper, lower = stack(pieces, axes)

    axes = "zx"
    swap = lambda value: shift(value, "c", 1)
    up = lambda value: shift(value, axes, 1)
    down = lambda value: shift(value, axes, 3)
    hold = lax.optimization_barrier
    upper_1, lower_3 = up(upper), down(lower)
    swapped = swap(block)
    products = multiply(weight, None, [(block, 0, 0), (block, 0, 1)], 0, axes)
    upper, lower, products = hold((upper, lower, products))
    upper_3, lower_1 = down(upper), up(lower)
    products = multiply(weight, products, [(swapped, 0, 0), (swapped, 0, 1)], 1, axes)
    upper_1, lower_3, products = hold((upper_1, lower_3, products))
    upper_2, lower_2 = up(upper_1), down(lower_3)
    pair_1 = swap(beside_each(upper_1, lower_3))
    products = multiply(weight, products, [(upper_1, 1, 0), (lower_3, 3, 1)], 0, axes)
    products = multiply(weight, products, [(upper_3, 3, 0), (lower_1, 1, 1)], 0, axes, cost=10)
    products = multiply(weight, products, [(pair_1, 1, 0), (pair_1, 3, 1)], 1, axes)
    upper_2, lower_2, upper_3, lower_1, products = hold((upper_2, lower_2, upper_3, lower_1, products))
    swapped_3 = swap(upper_3), swap(lower_1)
    swapped_2 = swap(upper_2), swap(lower_2)
    products = multiply(weight, products, [(upper_2, 2, 0), (lower_2, 2, 1)], 0, axes)
    products = multiply(weight, products, [(swapped_3[0], 3, 0), (swapped_3[1], 1, 1)], 1, axes)
    products = multiply(weight, products, [(swapped_2[0], 2, 0), (swapped_2[1], 2, 1)], 1, axes)

    weights, stats = join_halves(products, floor_stats, targets)
    sums, floor_sums = running_sums(weights, floors)
    group, before = stats, None
    for axis in ("c", "y", "z"):
        group, before = join(axis, group, before)
    (terms,) = join("x", group, before, last=(stats, totals.reshape(8, 128)))
    cumulative, bits = finish(sums, floor_sums, terms, entries)
    return cumulative.T, bits.reshape(1024)


def solution(mesh):
    in_specs = (P(STREAM, TENSOR), P(), P(None, BOTH), P(BOTH), P(), P())
    out_specs = (P(None, BOTH), P())
    return jax.shard_map(local, mesh=mesh, in_specs=in_specs, out_specs=out_specs, check_vma=False)
```

```python
import jax
import jax.numpy as jnp
from jax import lax
from jax.experimental import pallas as pl
from jax.experimental.pallas import tpu as pltpu
from jax.sharding import PartitionSpec as P

epsilon = 1e-05
STREAM, TENSOR = "stream", "tensor"
BOTH = (STREAM, TENSOR)
SIZES = {"x": 4, "z": 4, "y": 4, "c": 2}
STRIDES = {"x": 32, "z": 8, "y": 2, "c": 1}
ROWS = 8
VMEM = pl.BlockSpec(memory_space=pltpu.VMEM)


def coordinate(axis):
    index = lax.axis_index(STREAM) * 8 + lax.axis_index(TENSOR)
    return lax.rem(lax.div(index, STRIDES[axis]), SIZES[axis])


def shift(value, axis, hops, cross=False):
    pairs = []
    for source in range(128):
        name = axis[source % len(axis)]
        size, stride = SIZES[name], STRIDES[name]
        place = source // stride % size
        target = source + ((place + hops) % size - place) * stride
        pairs.append((source, target ^ 1 if cross else target))
    return lax.ppermute(value, BOTH, pairs)


def call(body, out_shape, name, inputs, vmem_mib=32, scratch=(), out_specs=VMEM, **rest):
    return pl.pallas_call(
        body,
        out_shape=out_shape,
        in_specs=[VMEM] * len(inputs),
        out_specs=out_specs,
        scratch_shapes=list(scratch),
        compiler_params=pltpu.CompilerParams(vmem_limit_bytes=vmem_mib << 20),
        name=name,
        **rest,
    )(*inputs)


def prepare(weight, hidden, floor_counts, gain, targets):
    entries = weight.shape[0]

    def body(weight_hbm, hidden_hbm, floors_hbm, gain_hbm, targets_hbm,
             weight_ref, hidden_ref, columns_ref, gain_out_ref, stats_ref,
             row, floors_ref, gain_ref, targets_ref, sems):
        copies = [
            pltpu.make_async_copy(source, target, sems.at[i])
            for i, (source, target) in enumerate((
                (floors_hbm, floors_ref),
                (targets_hbm, targets_ref),
                (gain_hbm, gain_ref),
                (hidden_hbm, hidden_ref),
                (weight_hbm.at[:, 0:4096], weight_ref),
            ))
        ]
        for copy in copies:
            copy.start()
        for copy in copies[:3]:
            copy.wait()
        row[...] = jnp.zeros_like(row)
        row[:, 0:entries] = jnp.broadcast_to(floors_ref[...].astype(jnp.float32), (8, entries))
        total = jnp.zeros((1, 128), jnp.float32)
        picked = [jnp.zeros((1, 128), jnp.float32)] * ROWS
        for b in range(ROWS):
            columns = jnp.transpose(jnp.concatenate([row[:, b * 128:(b + 1) * 128]] * 16, axis=0))
            columns_ref[b * 128:(b + 1) * 128, :] = columns
            total = total + jnp.sum(columns, axis=0, keepdims=True)
            rows = lax.broadcasted_iota(jnp.int32, (128, 128), 0) + (b * 128 + first_entry(entries))
            for j in range(ROWS):
                hit = jnp.where(rows == targets_ref[j:j + 1, :], columns, 0.0)
                picked[j] = picked[j] + jnp.sum(hit, axis=0, keepdims=True)
        stats_ref[0:8] = jnp.concatenate(picked, axis=0)
        stats_ref[8:16] = jnp.broadcast_to(total, (8, 128))
        gain_out_ref[...] = gain_ref[...].astype(jnp.float32).reshape(1, 8192)
        for copy in copies[3:]:
            copy.wait()

    anywhere = pl.BlockSpec(memory_space=pltpu.HBM)
    operands = (weight, hidden, floor_counts, gain, targets)
    return pl.pallas_call(
        body,
        out_shape=(
            pltpu.VMEM((entries, 4096), jnp.bfloat16),
            pltpu.VMEM(hidden.shape, jnp.bfloat16),
            pltpu.VMEM((1024, 128), jnp.float32),
            pltpu.VMEM((1, 8192), jnp.float32),
            pltpu.VMEM((16, 128), jnp.float32),
        ),
        in_specs=[anywhere] * 5,
        out_specs=(VMEM,) * 5,
        scratch_shapes=[
            pltpu.VMEM((8, 1024), jnp.float32),
            pltpu.VMEM((1, entries), jnp.int32),
            pltpu.VMEM((8192,), jnp.bfloat16),
            pltpu.VMEM((8, 128), jnp.int32),
            pltpu.SemaphoreType.DMA((5,)),
        ],
        compiler_params=pltpu.CompilerParams(vmem_limit_bytes=2 << 20),
        name="prepare",
    )(*(pltpu.with_memory_space_constraint(operand, pltpu.HBM) for operand in operands))


def load(weight):
    def body(weight_hbm, weight_ref, sem):
        copy = pltpu.make_async_copy(weight_hbm.at[:, 4096:8192], weight_ref, sem)
        copy.start()
        copy.wait()

    return pl.pallas_call(
        body,
        out_shape=pltpu.VMEM((weight.shape[0], 4096), jnp.bfloat16),
        in_specs=[pl.BlockSpec(memory_space=pltpu.HBM)],
        out_specs=VMEM,
        scratch_shapes=[pltpu.SemaphoreType.DMA],
        compiler_params=pltpu.CompilerParams(vmem_limit_bytes=2 << 20),
        name="load",
    )(pltpu.with_memory_space_constraint(weight, pltpu.HBM))


def first_entry(entries):
    return (lax.axis_index(STREAM) * 8 + lax.axis_index(TENSOR)) * entries


def join_halves(products, floor_stats, targets):
    entries = products.shape[2]

    def body(products_ref, floors_ref, targets_ref, weights_ref, stats_ref):
        core = lax.rem(lax.axis_index(TENSOR), 2)
        first = first_entry(entries)
        rows = lax.broadcasted_iota(jnp.int32, (entries, 128), 0)
        left = lax.broadcasted_iota(jnp.int32, (entries, 128), 1) < 64
        weights_ref[1000:1024, :] = jnp.zeros((24, 1024), jnp.float32)
        for j in range(ROWS):
            x, z = j // 2, j % 2 * 2
            near = slice(x // 2 * 128, x // 2 * 128 + 128)
            one, two = products_ref[core, z, :, near], products_ref[core, z + 1, :, near]
            if x % 2 == 0:
                two = pltpu.roll(two, 64, 1)
            else:
                one = pltpu.roll(one, 64, 1)
            tile = products_ref[1 - core, x, :, z * 64:z * 64 + 128] + jnp.where(left, one, two)
            peak = jnp.max(tile, axis=0, keepdims=True)
            exponent = jnp.exp(tile - peak)
            weights_ref[0:entries, j * 128:(j + 1) * 128] = exponent
            hit = rows == targets_ref[j:j + 1, :] - first
            stats_ref[j:j + 1, :] = peak
            stats_ref[8 + j:9 + j, :] = jnp.sum(exponent, axis=0, keepdims=True)
            stats_ref[16 + j:17 + j, :] = jnp.sum(jnp.where(hit, exponent, 0.0), axis=0, keepdims=True)
        stats_ref[24:40, :] = floors_ref[...]

    return call(
        body,
        (
            jax.ShapeDtypeStruct((1024, 1024), jnp.float32),
            jax.ShapeDtypeStruct((40, 128), jnp.float32),
        ),
        "join_halves",
        (products, floor_stats, targets),
        vmem_mib=6,
        out_specs=(VMEM, VMEM),
    )


def join(axis, stats, before, last=None):
    size = SIZES[axis]
    hops = [0, 1] if size == 2 else [0, 1, 3, 2]
    pieces = [stats] + [shift(stats, axis, k, axis != "c") for k in hops[1:]]

    def body(*refs):
        piece_refs, rest = refs[:size], refs[size:]
        if before is not None:
            before_ref, rest = rest[0], rest[1:]
        held = rest[-1]
        mine = coordinate(axis)
        for piece_ref, k in zip(piece_refs, hops):
            held[lax.rem(mine - k + size, size)] = piece_ref[...]
        peak = held[0, 0:8]
        for i in range(1, size):
            peak = jnp.maximum(peak, held[i, 0:8])
        mass = target = floor = total = jnp.zeros((8, 128), jnp.float32)
        mass_before = total_before = jnp.zeros((8, 128), jnp.float32)
        if before is not None:
            mass_before = before_ref[0:8] * jnp.exp(piece_refs[0][0:8] - peak)
            total_before = before_ref[8:16]
        for i in range(size):
            scale = jnp.exp(held[i, 0:8] - peak)
            part = held[i, 8:16] * scale
            mass = mass + part
            target = target + held[i, 16:24] * scale
            floor = floor + held[i, 24:32]
            total = total + held[i, 32:40]
            earlier = i < mine
            mass_before = mass_before + jnp.where(earlier, part, 0.0)
            total_before = total_before + jnp.where(earlier, held[i, 32:40], 0.0)
        if last is None:
            stats_ref, after_ref = rest[0], rest[1]
            stats_ref[0:8] = peak
            stats_ref[8:16] = mass
            stats_ref[16:24] = target
            stats_ref[24:32] = floor
            stats_ref[32:40] = total
            after_ref[0:8] = mass_before
            after_ref[8:16] = total_before
        else:
            own_ref, totals_ref, terms_ref = rest[:3]
            tokens = totals_ref[...].astype(jnp.float32)
            free = (tokens - total) / mass
            terms_ref[0:8] = jnp.exp(own_ref[0:8] - peak) * free / tokens
            terms_ref[8:16] = 1.0 / tokens
            terms_ref[16:24] = (total_before + mass_before * free) / tokens
            terms_ref[24:32] = -jnp.log2((floor + target * free) / tokens)

    inputs = pieces + ([] if before is None else [before]) + ([] if last is None else list(last))
    shapes = ((40, 128), (16, 128)) if last is None else ((32, 128),)
    return call(
        body,
        tuple(jax.ShapeDtypeStruct(shape, jnp.float32) for shape in shapes),
        "join_" + axis,
        inputs,
        vmem_mib=2,
        scratch=[pltpu.VMEM((size, 40, 128), jnp.float32)],
        out_specs=(VMEM,) * len(shapes),
    )


def running_sums(weights, floors):
    block = 256

    def body(weights_ref, floors_ref, sums_ref, floor_sums_ref):
        below = lax.broadcasted_iota(jnp.int32, (block, block), 1)
        lower = (below < lax.broadcasted_iota(jnp.int32, (block, block), 0)).astype(jnp.bfloat16)
        carry = [jnp.zeros((1, 256), jnp.float32)] * (ROWS // 2)
        floor_carry = jnp.zeros((1, 128), jnp.float32)
        for b in range(1024 // block):
            rows = slice(b * block, (b + 1) * block)
            floors = floors_ref[rows, :]
            floor_sums_ref[rows, :] = floor_carry + jnp.dot(
                lower, floors.astype(jnp.bfloat16), preferred_element_type=jnp.float32
            )
            floor_carry = floor_carry + jnp.sum(floors, axis=0, keepdims=True)
            for j in range(ROWS // 2):
                lanes = slice(j * 256, (j + 1) * 256)
                value = weights_ref[rows, lanes]
                high = value.astype(jnp.bfloat16)
                low = (value - high.astype(jnp.float32)).astype(jnp.bfloat16)
                sums = jnp.dot(lower, high, preferred_element_type=jnp.float32)
                sums = sums + jnp.dot(lower, low, preferred_element_type=jnp.float32)
                sums_ref[rows, lanes] = sums + carry[j]
                carry[j] = carry[j] + jnp.sum(value, axis=0, keepdims=True)

    return call(
        body,
        (
            jax.ShapeDtypeStruct((1024, 1024), jnp.float32),
            jax.ShapeDtypeStruct((1024, 128), jnp.float32),
        ),
        "running_sums",
        (weights, floors),
        vmem_mib=4,
        out_specs=(VMEM, VMEM),
    )


def finish(sums, floor_sums, terms, entries):
    def body(sums_ref, floors_ref, terms_ref, out_hbm, bits_hbm, out_ref, sems):
        copies = [pltpu.make_async_copy(terms_ref.at[24:32], bits_hbm, sems.at[ROWS])]
        copies[0].start()
        for j in range(ROWS):
            lanes = slice(j * 128, (j + 1) * 128)
            out_ref[:, lanes] = (
                sums_ref[0:entries, lanes] * terms_ref[j:j + 1, :]
                + floors_ref[0:entries, :] * terms_ref[8 + j:9 + j, :]
                + terms_ref[16 + j:17 + j, :]
            )
            copies.append(pltpu.make_async_copy(out_ref.at[:, lanes], out_hbm.at[:, lanes], sems.at[j]))
            copies[-1].start()
        for copy in copies:
            copy.wait()

    return call(
        body,
        (
            jax.ShapeDtypeStruct((entries, 1024), jnp.float32),
            jax.ShapeDtypeStruct((8, 128), jnp.float32),
        ),
        "finish",
        (sums, floor_sums, terms),
        vmem_mib=8,
        scratch=[pltpu.VMEM((entries, 1024), jnp.float32), pltpu.SemaphoreType.DMA((ROWS + 1,))],
        out_specs=(pl.BlockSpec(memory_space=pltpu.HBM),) * 2,
    )


def own_coordinate(axes):
    core = lax.rem(lax.axis_index(TENSOR), 2)
    return jnp.where(core == 0, coordinate(axes[0]), coordinate(axes[1]))


def square_sums(pieces):
    def body(*refs):
        mine = coordinate("y")
        total = jnp.zeros((64, 1), jnp.float32)
        for i, k in enumerate((0, 1, 3, 2)):
            piece = refs[i][...]
            place = lax.rem(mine - k + 4, 4)
            refs[4][:, pl.ds(pl.multiple_of(place * 1024, 1024), 1024)] = piece
            widened = piece.astype(jnp.float32)
            total = total + jnp.sum(widened * widened, axis=1, keepdims=True)
        refs[5][...] = jnp.broadcast_to(total, (64, 128))

    return call(
        body,
        (jax.ShapeDtypeStruct((64, 4096), jnp.bfloat16), jax.ShapeDtypeStruct((64, 128), jnp.float32)),
        "square_sums",
        pieces,
        vmem_mib=4,
        out_specs=(VMEM, VMEM),
    )


def normalize(features, own, other, gain):
    def body(features_ref, own_ref, other_ref, gain_ref, upper_ref, lower_ref):
        core = lax.rem(lax.axis_index(TENSOR), 2)
        mean_square = (own_ref[:, 0:1] + other_ref[:, 0:1]) * (1.0 / 8192)
        scale = lax.rsqrt(mean_square + epsilon)
        for y in range(4):
            lanes = slice(y * 1024, (y + 1) * 1024)
            row = gain_ref[:, pl.ds(pl.multiple_of((y * 2 + core) * 1024, 1024), 1024)]
            value = (features_ref[:, lanes].astype(jnp.float32) * scale * row).astype(jnp.bfloat16)
            upper_ref[:, lanes] = value[:32]
            lower_ref[:, lanes] = value[32:]

    shape = jax.ShapeDtypeStruct((32, 4096), jnp.bfloat16)
    return call(
        body,
        (shape, shape),
        "normalize",
        (features, own, other, gain),
        vmem_mib=4,
        out_specs=(VMEM, VMEM),
    )


def stack(pieces, axes):
    rows = 2 * pieces[0][2].shape[0]
    half = rows // 2

    def body(*refs):
        mine = own_coordinate(axes)
        for (side, hops, _), ref in zip(pieces, refs):
            place = lax.rem(mine + (4 - hops), 4)
            refs[-3][pl.ds(pl.multiple_of(place * rows + side * half, half), half), :] = ref[...]
            for i, out_ref in enumerate(refs[-2:]):

                @pl.when(place // 2 == i)
                def _():
                    at = pl.multiple_of((place - 2 * i) * rows + side * half, half)
                    out_ref[pl.ds(at, half), :] = ref[...]

    whole = jax.ShapeDtypeStruct((4 * rows, 4096), jnp.bfloat16)
    shape = jax.ShapeDtypeStruct((2 * rows, 4096), jnp.bfloat16)
    return call(
        body,
        (whole, shape, shape),
        "stack",
        [piece[2] for piece in pieces],
        vmem_mib=4,
        out_specs=(VMEM, VMEM, VMEM),
    )


def multiply(weight, products, pieces, side, axes, cost=1):
    entries = weight[0].shape[0]
    arrays = [pieces[0][0]] if pieces[0][0] is pieces[1][0] else [piece[0] for piece in pieces]
    inputs = list(weight) + ([] if products is None else [products]) + arrays

    def body(*refs):
        weight_refs, out_ref = refs[:2], refs[len(inputs)]
        token_refs = refs[len(inputs) - len(arrays):len(inputs)]
        core = lax.rem(lax.axis_index(TENSOR), 2)
        features = core if side == 0 else 1 - core
        mine = coordinate_of(features, axes)
        total = None
        for y in range(4):
            far = pl.ds(pl.multiple_of((y % 2 * 2 + features) * 1024, 1024), 1024)
            value = [ref[:, y * 1024:(y + 1) * 1024] for ref in token_refs]
            value = value[0] if len(value) == 1 else jnp.concatenate(value, axis=0)
            product = lax.dot_general(
                weight_refs[y // 2][:, far], value, (((1,), (1,)), ((), ())), preferred_element_type=jnp.float32
            )
            total = product if total is None else total + product
        for i, (_, hops, half) in enumerate(pieces):
            place = lax.rem(mine + (4 - hops), 4)
            out_ref[side, place, :, half * 128:half * 128 + 128] = total[:, i * 128:i * 128 + 128]

    shape = jax.ShapeDtypeStruct((2, 4, entries, 256), jnp.float32)
    return call(
        body,
        shape,
        "multiply",
        inputs,
        vmem_mib=6,
        input_output_aliases={} if products is None else {2: 0},
        cost_estimate=pl.CostEstimate(
            flops=cost * 2 * entries * 4096 * 256, bytes_accessed=4 << 20, transcendentals=0
        ),
    )


def beside_each(upper, lower):
    def body(upper_ref, lower_ref, out_ref):
        out_ref[0:128, :] = upper_ref[...]
        out_ref[128:256, :] = lower_ref[...]

    shape = jax.ShapeDtypeStruct((256, 4096), jnp.bfloat16)
    return call(body, shape, "beside_each", (upper, lower), vmem_mib=2)


def coordinate_of(core, axes):
    return jnp.where(core == 0, coordinate(axes[0]), coordinate(axes[1]))


def local(hidden, norm_gain, head_weight, floor_counts, totals, targets):
    weight = head_weight.T
    entries = weight.shape[0]
    targets = targets.reshape(8, 128)

    beside = [shift(hidden, "y", k) for k in (1, 3, 2)]
    first_half, hidden, floors, gain, floor_stats = prepare(
        weight, hidden, floor_counts.reshape(1, entries), norm_gain, targets
    )
    first_half, *beside = lax.optimization_barrier((first_half, *beside))
    raw, own = square_sums([hidden] + beside)
    upper, lower = normalize(raw, own, shift(own, "c", 1), gain)
    axes = "xz"
    upper_1, lower_3 = shift(upper, axes, 1), shift(lower, axes, 3)
    upper_3, lower_1 = shift(upper, axes, 3), shift(lower, axes, 1)
    upper_2, lower_2 = shift(upper_1, axes, 1), shift(lower_3, axes, 3)
    second_half, upper_3, lower_1 = lax.optimization_barrier((load(weight), upper_3, lower_1))
    weight = first_half, second_half
    pieces = [(0, 0, upper), (1, 0, lower), (0, 1, upper_1), (1, 3, lower_3)]
    pieces += [(0, 3, upper_3), (1, 1, lower_1), (0, 2, upper_2), (1, 2, lower_2)]
    block, upper, lower = stack(pieces, axes)

    axes = "zx"
    swap = lambda value: shift(value, "c", 1)
    up = lambda value: shift(value, axes, 1)
    down = lambda value: shift(value, axes, 3)
    hold = lax.optimization_barrier
    upper_1, lower_3 = up(upper), down(lower)
    swapped = swap(block)
    products = multiply(weight, None, [(block, 0, 0), (block, 0, 1)], 0, axes)
    upper, lower, products = hold((upper, lower, products))
    upper_3, lower_1 = down(upper), up(lower)
    products = multiply(weight, products, [(swapped, 0, 0), (swapped, 0, 1)], 1, axes)
    upper_1, lower_3, products = hold((upper_1, lower_3, products))
    upper_2, lower_2 = up(upper_1), down(lower_3)
    pair_1 = swap(beside_each(upper_1, lower_3))
    products = multiply(weight, products, [(upper_1, 1, 0), (lower_3, 3, 1)], 0, axes)
    products = multiply(weight, products, [(upper_3, 3, 0), (lower_1, 1, 1)], 0, axes, cost=10)
    products = multiply(weight, products, [(pair_1, 1, 0), (pair_1, 3, 1)], 1, axes)
    upper_2, lower_2, upper_3, lower_1, products = hold((upper_2, lower_2, upper_3, lower_1, products))
    swapped_3 = swap(upper_3), swap(lower_1)
    swapped_2 = swap(upper_2), swap(lower_2)
    products = multiply(weight, products, [(upper_2, 2, 0), (lower_2, 2, 1)], 0, axes)
    products = multiply(weight, products, [(swapped_3[0], 3, 0), (swapped_3[1], 1, 1)], 1, axes)
    products = multiply(weight, products, [(swapped_2[0], 2, 0), (swapped_2[1], 2, 1)], 1, axes)

    weights, stats = join_halves(products, floor_stats, targets)
    sums, floor_sums = running_sums(weights, floors)
    group, before = stats, None
    for axis in ("c", "y", "z"):
        group, before = join(axis, group, before)
    (terms,) = join("x", group, before, last=(stats, totals.reshape(8, 128)))
    cumulative, bits = finish(sums, floor_sums, terms, entries)
    return cumulative.T, bits.reshape(1024)


def solution(mesh):
    in_specs = (P(STREAM, TENSOR), P(), P(None, BOTH), P(BOTH), P(), P())
    out_specs = (P(None, BOTH), P())
    return jax.shard_map(local, mesh=mesh, in_specs=in_specs, out_specs=out_specs, check_vma=False)
```

```python
import jax
import jax.numpy as jnp
from jax import lax
from jax.experimental import pallas as pl
from jax.experimental.pallas import tpu as pltpu
from jax.sharding import PartitionSpec as P

epsilon = 1e-05
STREAM, TENSOR = "stream", "tensor"
BOTH = (STREAM, TENSOR)
SIZES = {"x": 4, "z": 4, "y": 4, "c": 2}
STRIDES = {"x": 32, "z": 8, "y": 2, "c": 1}
ROWS = 8
VMEM = pl.BlockSpec(memory_space=pltpu.VMEM)


def coordinate(axis):
    index = lax.axis_index(STREAM) * 8 + lax.axis_index(TENSOR)
    return lax.rem(lax.div(index, STRIDES[axis]), SIZES[axis])


def shift(value, axis, hops, cross=False):
    pairs = []
    for source in range(128):
        name = axis[source % len(axis)]
        size, stride = SIZES[name], STRIDES[name]
        place = source // stride % size
        target = source + ((place + hops) % size - place) * stride
        pairs.append((source, target ^ 1 if cross else target))
    return lax.ppermute(value, BOTH, pairs)


def call(body, out_shape, name, inputs, vmem_mib=32, scratch=(), out_specs=VMEM, **rest):
    return pl.pallas_call(
        body,
        out_shape=out_shape,
        in_specs=[VMEM] * len(inputs),
        out_specs=out_specs,
        scratch_shapes=list(scratch),
        compiler_params=pltpu.CompilerParams(vmem_limit_bytes=vmem_mib << 20),
        name=name,
        **rest,
    )(*inputs)


def prepare(weight, hidden, floor_counts, gain, targets):
    entries = weight.shape[0]

    def body(weight_hbm, hidden_hbm, floors_hbm, gain_hbm, targets_hbm,
             weight_ref, hidden_ref, columns_ref, gain_out_ref, stats_ref,
             row, floors_ref, gain_ref, targets_ref, sems):
        copies = [
            pltpu.make_async_copy(source, target, sems.at[i])
            for i, (source, target) in enumerate((
                (floors_hbm, floors_ref),
                (targets_hbm, targets_ref),
                (gain_hbm, gain_ref),
                (hidden_hbm, hidden_ref),
                (weight_hbm.at[:, 0:4096], weight_ref),
            ))
        ]
        for copy in copies:
            copy.start()
        for copy in copies[:3]:
            copy.wait()
        row[...] = jnp.zeros_like(row)
        row[:, 0:entries] = jnp.broadcast_to(floors_ref[...].astype(jnp.float32), (8, entries))
        total = jnp.zeros((1, 128), jnp.float32)
        picked = [jnp.zeros((1, 128), jnp.float32)] * ROWS
        for b in range(ROWS):
            columns = jnp.transpose(jnp.concatenate([row[:, b * 128:(b + 1) * 128]] * 16, axis=0))
            columns_ref[b * 128:(b + 1) * 128, :] = columns
            total = total + jnp.sum(columns, axis=0, keepdims=True)
            rows = lax.broadcasted_iota(jnp.int32, (128, 128), 0) + (b * 128 + first_entry(entries))
            for j in range(ROWS):
                hit = jnp.where(rows == targets_ref[j:j + 1, :], columns, 0.0)
                picked[j] = picked[j] + jnp.sum(hit, axis=0, keepdims=True)
        stats_ref[0:8] = jnp.concatenate(picked, axis=0)
        stats_ref[8:16] = jnp.broadcast_to(total, (8, 128))
        gain_out_ref[...] = gain_ref[...].astype(jnp.float32).reshape(1, 8192)
        for copy in copies[3:]:
            copy.wait()

    anywhere = pl.BlockSpec(memory_space=pltpu.HBM)
    operands = (weight, hidden, floor_counts, gain, targets)
    return pl.pallas_call(
        body,
        out_shape=(
            pltpu.VMEM((entries, 4096), jnp.bfloat16),
            pltpu.VMEM(hidden.shape, jnp.bfloat16),
            pltpu.VMEM((1024, 128), jnp.float32),
            pltpu.VMEM((1, 8192), jnp.float32),
            pltpu.VMEM((16, 128), jnp.float32),
        ),
        in_specs=[anywhere] * 5,
        out_specs=(VMEM,) * 5,
        scratch_shapes=[
            pltpu.VMEM((8, 1024), jnp.float32),
            pltpu.VMEM((1, entries), jnp.int32),
            pltpu.VMEM((8192,), jnp.bfloat16),
            pltpu.VMEM((8, 128), jnp.int32),
            pltpu.SemaphoreType.DMA((5,)),
        ],
        compiler_params=pltpu.CompilerParams(vmem_limit_bytes=2 << 20),
        name="prepare",
    )(*(pltpu.with_memory_space_constraint(operand, pltpu.HBM) for operand in operands))


def load(weight):
    def body(weight_hbm, weight_ref, sem):
        copy = pltpu.make_async_copy(weight_hbm.at[:, 4096:8192], weight_ref, sem)
        copy.start()
        copy.wait()

    return pl.pallas_call(
        body,
        out_shape=pltpu.VMEM((weight.shape[0], 4096), jnp.bfloat16),
        in_specs=[pl.BlockSpec(memory_space=pltpu.HBM)],
        out_specs=VMEM,
        scratch_shapes=[pltpu.SemaphoreType.DMA],
        compiler_params=pltpu.CompilerParams(vmem_limit_bytes=2 << 20),
        name="load",
    )(pltpu.with_memory_space_constraint(weight, pltpu.HBM))


def first_entry(entries):
    return (lax.axis_index(STREAM) * 8 + lax.axis_index(TENSOR)) * entries


def join_halves(products, floor_stats, targets):
    entries = products.shape[2]

    def body(products_ref, floors_ref, targets_ref, weights_ref, stats_ref):
        core = lax.rem(lax.axis_index(TENSOR), 2)
        first = first_entry(entries)
        rows = lax.broadcasted_iota(jnp.int32, (entries, 128), 0)
        left = lax.broadcasted_iota(jnp.int32, (entries, 128), 1) < 64
        weights_ref[1000:1024, :] = jnp.zeros((24, 1024), jnp.float32)
        for j in range(ROWS):
            x, z = j // 2, j % 2 * 2
            near = slice(x // 2 * 128, x // 2 * 128 + 128)
            one, two = products_ref[core, z, :, near], products_ref[core, z + 1, :, near]
            if x % 2 == 0:
                two = pltpu.roll(two, 64, 1)
            else:
                one = pltpu.roll(one, 64, 1)
            tile = products_ref[1 - core, x, :, z * 64:z * 64 + 128] + jnp.where(left, one, two)
            peak = jnp.max(tile, axis=0, keepdims=True)
            exponent = jnp.exp(tile - peak)
            weights_ref[0:entries, j * 128:(j + 1) * 128] = exponent
            hit = rows == targets_ref[j:j + 1, :] - first
            stats_ref[j:j + 1, :] = peak
            stats_ref[8 + j:9 + j, :] = jnp.sum(exponent, axis=0, keepdims=True)
            stats_ref[16 + j:17 + j, :] = jnp.sum(jnp.where(hit, exponent, 0.0), axis=0, keepdims=True)
        stats_ref[24:40, :] = floors_ref[...]

    return call(
        body,
        (
            jax.ShapeDtypeStruct((1024, 1024), jnp.float32),
            jax.ShapeDtypeStruct((40, 128), jnp.float32),
        ),
        "join_halves",
        (products, floor_stats, targets),
        vmem_mib=6,
        out_specs=(VMEM, VMEM),
    )


def join(axis, stats, before, last=None):
    size = SIZES[axis]
    hops = [0, 1] if size == 2 else [0, 3, 1, 2]
    pieces = [stats] + [shift(stats, axis, k, axis != "c") for k in hops[1:]]

    def body(*refs):
        piece_refs, rest = refs[:size], refs[size:]
        if before is not None:
            before_ref, rest = rest[0], rest[1:]
        held = rest[-1]
        mine = coordinate(axis)
        for piece_ref, k in zip(piece_refs, hops):
            held[lax.rem(mine - k + size, size)] = piece_ref[...]
        peak = held[0, 0:8]
        for i in range(1, size):
            peak = jnp.maximum(peak, held[i, 0:8])
        mass = target = floor = total = jnp.zeros((8, 128), jnp.float32)
        mass_before = total_before = jnp.zeros((8, 128), jnp.float32)
        if before is not None:
            mass_before = before_ref[0:8] * jnp.exp(piece_refs[0][0:8] - peak)
            total_before = before_ref[8:16]
        for i in range(size):
            scale = jnp.exp(held[i, 0:8] - peak)
            part = held[i, 8:16] * scale
            mass = mass + part
            target = target + held[i, 16:24] * scale
            floor = floor + held[i, 24:32]
            total = total + held[i, 32:40]
            earlier = i < mine
            mass_before = mass_before + jnp.where(earlier, part, 0.0)
            total_before = total_before + jnp.where(earlier, held[i, 32:40], 0.0)
        if last is None:
            stats_ref, after_ref = rest[0], rest[1]
            stats_ref[0:8] = peak
            stats_ref[8:16] = mass
            stats_ref[16:24] = target
            stats_ref[24:32] = floor
            stats_ref[32:40] = total
            after_ref[0:8] = mass_before
            after_ref[8:16] = total_before
        else:
            own_ref, totals_ref, terms_ref = rest[:3]
            tokens = totals_ref[...].astype(jnp.float32)
            free = (tokens - total) / mass
            terms_ref[0:8] = jnp.exp(own_ref[0:8] - peak) * free / tokens
            terms_ref[8:16] = 1.0 / tokens
            terms_ref[16:24] = (total_before + mass_before * free) / tokens
            terms_ref[24:32] = -jnp.log2((floor + target * free) / tokens)

    inputs = pieces + ([] if before is None else [before]) + ([] if last is None else list(last))
    shapes = ((40, 128), (16, 128)) if last is None else ((32, 128),)
    return call(
        body,
        tuple(jax.ShapeDtypeStruct(shape, jnp.float32) for shape in shapes),
        "join_" + axis,
        inputs,
        vmem_mib=2,
        scratch=[pltpu.VMEM((size, 40, 128), jnp.float32)],
        out_specs=(VMEM,) * len(shapes),
    )


def running_sums(weights, floors):
    block = 256

    def body(weights_ref, floors_ref, sums_ref, floor_sums_ref):
        below = lax.broadcasted_iota(jnp.int32, (block, block), 1)
        lower = (below < lax.broadcasted_iota(jnp.int32, (block, block), 0)).astype(jnp.bfloat16)
        carry = [jnp.zeros((1, 256), jnp.float32)] * (ROWS // 2)
        floor_carry = jnp.zeros((1, 128), jnp.float32)
        for b in range(1024 // block):
            rows = slice(b * block, (b + 1) * block)
            floors = floors_ref[rows, :]
            floor_sums_ref[rows, :] = floor_carry + jnp.dot(
                lower, floors.astype(jnp.bfloat16), preferred_element_type=jnp.float32
            )
            floor_carry = floor_carry + jnp.sum(floors, axis=0, keepdims=True)
            for j in range(ROWS // 2):
                lanes = slice(j * 256, (j + 1) * 256)
                value = weights_ref[rows, lanes]
                high = value.astype(jnp.bfloat16)
                low = (value - high.astype(jnp.float32)).astype(jnp.bfloat16)
                sums = jnp.dot(lower, high, preferred_element_type=jnp.float32)
                sums = sums + jnp.dot(lower, low, preferred_element_type=jnp.float32)
                sums_ref[rows, lanes] = sums + carry[j]
                carry[j] = carry[j] + jnp.sum(value, axis=0, keepdims=True)

    return call(
        body,
        (
            jax.ShapeDtypeStruct((1024, 1024), jnp.float32),
            jax.ShapeDtypeStruct((1024, 128), jnp.float32),
        ),
        "running_sums",
        (weights, floors),
        vmem_mib=4,
        out_specs=(VMEM, VMEM),
    )


def finish(sums, floor_sums, terms, entries):
    def body(sums_ref, floors_ref, terms_ref, out_hbm, bits_hbm, out_ref, sems):
        copies = [pltpu.make_async_copy(terms_ref.at[24:32], bits_hbm, sems.at[ROWS])]
        copies[0].start()
        for j in range(ROWS):
            lanes = slice(j * 128, (j + 1) * 128)
            out_ref[:, lanes] = (
                sums_ref[0:entries, lanes] * terms_ref[j:j + 1, :]
                + floors_ref[0:entries, :] * terms_ref[8 + j:9 + j, :]
                + terms_ref[16 + j:17 + j, :]
            )
            copies.append(pltpu.make_async_copy(out_ref.at[:, lanes], out_hbm.at[:, lanes], sems.at[j]))
            copies[-1].start()
        for copy in copies:
            copy.wait()

    return call(
        body,
        (
            jax.ShapeDtypeStruct((entries, 1024), jnp.float32),
            jax.ShapeDtypeStruct((8, 128), jnp.float32),
        ),
        "finish",
        (sums, floor_sums, terms),
        vmem_mib=8,
        scratch=[pltpu.VMEM((entries, 1024), jnp.float32), pltpu.SemaphoreType.DMA((ROWS + 1,))],
        out_specs=(pl.BlockSpec(memory_space=pltpu.HBM),) * 2,
    )


def own_coordinate(axes):
    core = lax.rem(lax.axis_index(TENSOR), 2)
    return jnp.where(core == 0, coordinate(axes[0]), coordinate(axes[1]))


def square_sums(pieces):
    def body(*refs):
        mine = coordinate("y")
        total = jnp.zeros((64, 1), jnp.float32)
        for i, k in enumerate((0, 1, 3, 2)):
            piece = refs[i][...]
            place = lax.rem(mine - k + 4, 4)
            refs[4][:, pl.ds(pl.multiple_of(place * 1024, 1024), 1024)] = piece
            widened = piece.astype(jnp.float32)
            total = total + jnp.sum(widened * widened, axis=1, keepdims=True)
        refs[5][...] = jnp.broadcast_to(total, (64, 128))

    return call(
        body,
        (jax.ShapeDtypeStruct((64, 4096), jnp.bfloat16), jax.ShapeDtypeStruct((64, 128), jnp.float32)),
        "square_sums",
        pieces,
        vmem_mib=4,
        out_specs=(VMEM, VMEM),
    )


def normalize(features, own, other, gain):
    def body(features_ref, own_ref, other_ref, gain_ref, upper_ref, lower_ref):
        core = lax.rem(lax.axis_index(TENSOR), 2)
        mean_square = (own_ref[:, 0:1] + other_ref[:, 0:1]) * (1.0 / 8192)
        scale = lax.rsqrt(mean_square + epsilon)
        for y in range(4):
            lanes = slice(y * 1024, (y + 1) * 1024)
            row = gain_ref[:, pl.ds(pl.multiple_of((y * 2 + core) * 1024, 1024), 1024)]
            value = (features_ref[:, lanes].astype(jnp.float32) * scale * row).astype(jnp.bfloat16)
            upper_ref[:, lanes] = value[:32]
            lower_ref[:, lanes] = value[32:]

    shape = jax.ShapeDtypeStruct((32, 4096), jnp.bfloat16)
    return call(
        body,
        (shape, shape),
        "normalize",
        (features, own, other, gain),
        vmem_mib=4,
        out_specs=(VMEM, VMEM),
    )


def stack(pieces, axes):
    rows = 2 * pieces[0][2].shape[0]
    half = rows // 2

    def body(*refs):
        mine = own_coordinate(axes)
        for (side, hops, _), ref in zip(pieces, refs):
            place = lax.rem(mine + (4 - hops), 4)
            refs[-3][pl.ds(pl.multiple_of(place * rows + side * half, half), half), :] = ref[...]
            for i, out_ref in enumerate(refs[-2:]):

                @pl.when(place // 2 == i)
                def _():
                    at = pl.multiple_of((place - 2 * i) * rows + side * half, half)
                    out_ref[pl.ds(at, half), :] = ref[...]

    whole = jax.ShapeDtypeStruct((4 * rows, 4096), jnp.bfloat16)
    shape = jax.ShapeDtypeStruct((2 * rows, 4096), jnp.bfloat16)
    return call(
        body,
        (whole, shape, shape),
        "stack",
        [piece[2] for piece in pieces],
        vmem_mib=4,
        out_specs=(VMEM, VMEM, VMEM),
    )


def multiply(weight, products, pieces, side, axes, cost=1):
    entries = weight[0].shape[0]
    arrays = [pieces[0][0]] if pieces[0][0] is pieces[1][0] else [piece[0] for piece in pieces]
    inputs = list(weight) + ([] if products is None else [products]) + arrays

    def body(*refs):
        weight_refs, out_ref = refs[:2], refs[len(inputs)]
        token_refs = refs[len(inputs) - len(arrays):len(inputs)]
        core = lax.rem(lax.axis_index(TENSOR), 2)
        features = core if side == 0 else 1 - core
        mine = coordinate_of(features, axes)
        total = None
        for y in range(4):
            far = pl.ds(pl.multiple_of((y % 2 * 2 + features) * 1024, 1024), 1024)
            value = [ref[:, y * 1024:(y + 1) * 1024] for ref in token_refs]
            value = value[0] if len(value) == 1 else jnp.concatenate(value, axis=0)
            product = lax.dot_general(
                weight_refs[y // 2][:, far], value, (((1,), (1,)), ((), ())), preferred_element_type=jnp.float32
            )
            total = product if total is None else total + product
        for i, (_, hops, half) in enumerate(pieces):
            place = lax.rem(mine + (4 - hops), 4)
            out_ref[side, place, :, half * 128:half * 128 + 128] = total[:, i * 128:i * 128 + 128]

    shape = jax.ShapeDtypeStruct((2, 4, entries, 256), jnp.float32)
    return call(
        body,
        shape,
        "multiply",
        inputs,
        vmem_mib=6,
        input_output_aliases={} if products is None else {2: 0},
        cost_estimate=pl.CostEstimate(
            flops=cost * 2 * entries * 4096 * 256, bytes_accessed=4 << 20, transcendentals=0
        ),
    )


def beside_each(upper, lower):
    def body(upper_ref, lower_ref, out_ref):
        out_ref[0:128, :] = upper_ref[...]
        out_ref[128:256, :] = lower_ref[...]

    shape = jax.ShapeDtypeStruct((256, 4096), jnp.bfloat16)
    return call(body, shape, "beside_each", (upper, lower), vmem_mib=2)


def coordinate_of(core, axes):
    return jnp.where(core == 0, coordinate(axes[0]), coordinate(axes[1]))


def local(hidden, norm_gain, head_weight, floor_counts, totals, targets):
    weight = head_weight.T
    entries = weight.shape[0]
    targets = targets.reshape(8, 128)

    beside = [shift(hidden, "y", k) for k in (1, 3, 2)]
    first_half, hidden, floors, gain, floor_stats = prepare(
        weight, hidden, floor_counts.reshape(1, entries), norm_gain, targets
    )
    first_half, *beside = lax.optimization_barrier((first_half, *beside))
    raw, own = square_sums([hidden] + beside)
    upper, lower = normalize(raw, own, shift(own, "c", 1), gain)
    axes = "xz"
    upper_1, lower_3 = shift(upper, axes, 1), shift(lower, axes, 3)
    upper_3, lower_1 = shift(upper, axes, 3), shift(lower, axes, 1)
    upper_2, lower_2 = shift(upper_1, axes, 1), shift(lower_3, axes, 3)
    second_half, upper_3, lower_1 = lax.optimization_barrier((load(weight), upper_3, lower_1))
    weight = first_half, second_half
    pieces = [(0, 0, upper), (1, 0, lower), (0, 1, upper_1), (1, 3, lower_3)]
    pieces += [(0, 3, upper_3), (1, 1, lower_1), (0, 2, upper_2), (1, 2, lower_2)]
    block, upper, lower = stack(pieces, axes)

    axes = "zx"
    swap = lambda value: shift(value, "c", 1)
    up = lambda value: shift(value, axes, 1)
    down = lambda value: shift(value, axes, 3)
    hold = lax.optimization_barrier
    upper_1, lower_3 = up(upper), down(lower)
    swapped = swap(block)
    products = multiply(weight, None, [(block, 0, 0), (block, 0, 1)], 0, axes)
    upper, lower, products = hold((upper, lower, products))
    upper_3, lower_1 = down(upper), up(lower)
    products = multiply(weight, products, [(swapped, 0, 0), (swapped, 0, 1)], 1, axes)
    upper_1, lower_3, products = hold((upper_1, lower_3, products))
    upper_2, lower_2 = up(upper_1), down(lower_3)
    pair_1 = swap(beside_each(upper_1, lower_3))
    products = multiply(weight, products, [(upper_1, 1, 0), (lower_3, 3, 1)], 0, axes)
    products = multiply(weight, products, [(upper_3, 3, 0), (lower_1, 1, 1)], 0, axes, cost=10)
    products = multiply(weight, products, [(pair_1, 1, 0), (pair_1, 3, 1)], 1, axes)
    upper_2, lower_2, upper_3, lower_1, products = hold((upper_2, lower_2, upper_3, lower_1, products))
    swapped_3 = swap(upper_3), swap(lower_1)
    swapped_2 = swap(upper_2), swap(lower_2)
    products = multiply(weight, products, [(upper_2, 2, 0), (lower_2, 2, 1)], 0, axes)
    products = multiply(weight, products, [(swapped_3[0], 3, 0), (swapped_3[1], 1, 1)], 1, axes)
    products = multiply(weight, products, [(swapped_2[0], 2, 0), (swapped_2[1], 2, 1)], 1, axes)

    weights, stats = join_halves(products, floor_stats, targets)
    sums, floor_sums = running_sums(weights, floors)
    group, before = stats, None
    for axis in ("c", "y", "z"):
        group, before = join(axis, group, before)
    (terms,) = join("x", group, before, last=(stats, totals.reshape(8, 128)))
    cumulative, bits = finish(sums, floor_sums, terms, entries)
    return cumulative.T, bits.reshape(1024)


def solution(mesh):
    in_specs = (P(STREAM, TENSOR), P(), P(None, BOTH), P(BOTH), P(), P())
    out_specs = (P(None, BOTH), P())
    return jax.shard_map(local, mesh=mesh, in_specs=in_specs, out_specs=out_specs, check_vma=False)
```
